512 devices in a mesh: gx: 8 (over z), gy: 8 (over y), gz: 8 (over x, core).
Axes of the slice: x: 4, y: 8, z: 8, core: 2. Of those that a mesh axis runs over, the one named last changes fastest.
Arguments:
- panel_in: bfloat16 [32, 64, 64, 1024], P(None, 'gx', 'gy', 'gz'), may hold values from -9 to 9
- prior_modes: bfloat16 [64, 64, 64, 1024], P(None, 'gx', 'gy', 'gz'), may hold values from -9 to 9, as said below
- stiffness: bfloat16 [64, 64, 1024], P('gx', 'gy', 'gz'), may hold values from 0.5 to 4
- mass_shift: bfloat16 [64, 64, 1024], P('gx', 'gy', 'gz'), may hold values from 2 to 16
Outputs:
- filtered_basis: bfloat16 [32, 64, 64, 1024], P(None, 'gx', 'gy', 'gz')
- upper_factor: float32 [32, 32], replicated
The draws below stay inside these ranges and needn't reach their ends.
Inputs may be any that keep to these rules, and one draw needn't show every extreme that they name: `prior_modes`: orthonormal under the sum over nodes of products divided by 4194304.
All inputs are finite; a program needn't handle non-finite values.
Results may differ from the reference program's by a relative error of at most 0.0089.
The reference program's roundings to bfloat16 on the way count: a program that leaves them out, or rounds other values in their place, can miss the bound.
Values may be sent and summed in bfloat16 or wider, within the bound.
A program may use at most 128 MiB of HBM per device.

```python
import math
import jax
import jax.numpy as jnp
import numpy as np
from jax import lax

VECS = 32
PRIOR = 64
NX = 64
NY = 64
NZ = 1024
NODES = 4194304


common_count = 8


def walsh_modes(key, first_index):
    signs = jnp.where(jax.random.bernoulli(key, 0.5, (NODES,)), 1.0, -1.0).astype(jnp.float32)
    node_index = jnp.arange(NODES, dtype=jnp.int32)
    pattern_index = jnp.arange(PRIOR, dtype=jnp.int32) + first_index
    parity = pattern_index[:, None] & node_index[None, :]
    parity = parity ^ parity >> 16
    parity = parity ^ parity >> 8
    parity = parity ^ parity >> 4
    parity = parity ^ parity >> 2
    parity = parity ^ parity >> 1
    parity = parity & 1
    return signs[None, :] * (1.0 - 2.0 * parity.astype(jnp.float32))


def draw_prior_modes(key, part):
    modes = walsh_modes(key, 1)
    return modes.reshape(PRIOR, NX, NY, NZ).astype(jnp.bfloat16)


def draw_panel_in(key, part):
    modes = walsh_modes(key, 1)
    key = jax.random.fold_in(key, 23)
    key_mix, key_common, key_load, key_noise = jax.random.split(key, 4)
    loads = jnp.clip(jax.random.normal(key_load, (VECS, common_count), jnp.float32), -4.0, 4.0)
    mixing = jnp.clip(jax.random.normal(key_mix, (VECS, PRIOR), jnp.float32), -4.0, 4.0)
    common = jnp.clip(jax.random.normal(key_common, (common_count, NODES), jnp.float32), -5.0, 5.0)
    noise = jnp.clip(jax.random.normal(key_noise, (VECS, NODES), jnp.float32), -5.0, 5.0)
    spanned = jnp.dot(mixing, modes, precision=lax.Precision.HIGHEST) / PRIOR ** 0.5
    shared = jnp.dot(loads, common, precision=lax.Precision.HIGHEST) / common_count ** 0.5
    mixed = 0.8 * spanned + 0.4 * shared + 0.45 * noise
    return jnp.clip(mixed, -9.0, 9.0).reshape(VECS, NX, NY, NZ).astype(jnp.bfloat16)


def shard_levels(key, dims, cuts, least, top_value):
    def one(dim, shards_of):
        steps = jax.random.uniform(jax.random.fold_in(jax.random.fold_in(key, 6), dim), (shards_of,), jnp.float32, least / len(cuts), top_value / len(cuts))
        return jnp.repeat(jnp.exp(steps), dims[dim] // shards_of).reshape((-1,) + (1,) * (len(dims) - dim - 1))

    loudness = one(*cuts[0])
    for cut in cuts[1:]:
        loudness = loudness * one(*cut)
    return loudness


def setup_inputs(seed: int = 0) -> dict:
    key_list = jax.random.split(jax.random.key(seed), 5)
    return {
        "panel_in": draw_panel_in(jax.random.fold_in(key_list[4], 71), 0),
        "prior_modes": draw_prior_modes(jax.random.fold_in(key_list[4], 71), 0),
        "stiffness": jnp.clip(jnp.exp(math.log(4.0) - 2.0794415 * jax.random.uniform(key_list[2], (NX, NY, NZ), jnp.float32) ** shard_levels(key_list[2], (NX, NY, NZ), ((0, 8), (1, 8), (2, 8)), -0.2, 0.2)), 0.5, 4.0).astype(jnp.bfloat16),
        "mass_shift": jnp.clip(jnp.exp(math.log(16.0) - 2.0794415 * jax.random.uniform(key_list[3], (NX, NY, NZ), jnp.float32) ** shard_levels(key_list[3], (NX, NY, NZ), ((0, 8), (1, 8), (2, 8)), -0.2, 0.2)), 2.0, 16.0).astype(jnp.bfloat16),
    }


filter_center = 10.0
filter_half = 12.0

def lobatto_tables():
    points = np.array([-1.0, -np.sqrt(3.0 / 7.0), 0.0, np.sqrt(3.0 / 7.0), 1.0])
    weights = np.array([0.1, 49.0 / 90.0, 32.0 / 45.0, 49.0 / 90.0, 0.1])
    scales = np.array([np.prod([points[i] - points[k] for k in range(5) if k != i]) for i in range(5)])
    derivative = np.zeros((5, 5))
    for i in range(5):
        for j in range(5):
            if j != i:
                derivative[i, j] = scales[i] / scales[j] / (points[i] - points[j])
        derivative[i, i] = -np.sum(derivative[i])
    return (derivative, weights)

def node_weights(length):
    derivative, weights = lobatto_tables()
    summed = np.zeros(length)
    for m in range((length - 1) // 4):
        summed[4 * m:4 * m + 5] += weights
    return summed

def to_elements(leading, elements):
    first_four = leading[:4 * elements].reshape((elements, 4) + leading.shape[1:])
    tail_node = leading[4:4 * elements + 1:4][:, None]
    return jnp.concatenate([first_four, tail_node], axis=1)

def from_elements(local_vals, length):
    elements = local_vals.shape[0]
    trailing = local_vals.shape[2:]
    summed = jnp.zeros((length,) + trailing, local_vals.dtype)
    summed = summed.at[:4 * elements].add(local_vals[:, :4].reshape((4 * elements,) + trailing))
    return summed.at[4:4 * elements + 1:4].add(local_vals[:, 4])

def stiff_term(fields, stiff_field, axis_num, offset, extents, derivative, weights, node_ws):
    windows = [slice(offset, offset + extents[k]) for k in range(3)]
    windows[axis_num] = slice(None)
    values = jnp.moveaxis(fields[tuple(windows)], axis_num, 0)
    kappas = jnp.moveaxis(stiff_field[tuple(windows)], axis_num, 0)
    length = values.shape[0]
    elements = (length - 1) // 4
    local_vals = to_elements(values, elements).astype(jnp.float32)
    local_kappa = to_elements(kappas, elements).astype(jnp.float32)
    slopes = jnp.einsum('qa,mars->mqrs', derivative, local_vals)
    others = [node_ws[k][offset:offset + extents[k]] for k in range(3) if k != axis_num]
    factor = weights[None, :, None, None] * local_kappa * others[0][None, None, :, None] * others[1][None, None, None, :]
    fluxes = (slopes * factor).astype(jnp.bfloat16)
    fluxes = lax.optimization_barrier(fluxes).astype(jnp.float32)
    backward = jnp.einsum('qa,mqrs->mars', derivative, fluxes)
    assembled = from_elements(backward, length)[offset:offset + extents[axis_num]]
    return jnp.moveaxis(assembled, 0, axis_num)

def apply_one(fields, stiff_field, mass_field, halo_width, keep_width):
    derivative, weights = lobatto_tables()
    derivative = lax.optimization_barrier(jnp.asarray(derivative, jnp.float32).astype(jnp.bfloat16)).astype(jnp.float32)
    weights = jnp.asarray(weights, jnp.float32)
    offset = halo_width - keep_width
    extents = [fields.shape[k] - 2 * offset for k in range(3)]
    node_ws = [jnp.asarray(node_weights(fields.shape[k]), jnp.float32) for k in range(3)]
    result = stiff_term(fields, stiff_field, 0, offset, extents, derivative, weights, node_ws)
    result = result + stiff_term(fields, stiff_field, 1, offset, extents, derivative, weights, node_ws)
    result = result + stiff_term(fields, stiff_field, 2, offset, extents, derivative, weights, node_ws)
    centre = tuple((slice(offset, offset + extents[k]) for k in range(3)))
    volume = node_ws[0][centre[0]][:, None, None] * node_ws[1][centre[1]][None, :, None] * node_ws[2][centre[2]][None, None, :]
    mass_term = volume * mass_field[centre].astype(jnp.float32) * fields[centre].astype(jnp.float32)
    return result - mass_term

def reference(panel_in, prior_modes, stiffness, mass_shift):
    stiff_pad = jnp.pad(stiffness, 3)
    mass_pad = jnp.pad(mass_shift, 3)

    def operate_all(fields):
        return lax.map(lambda f: apply_one(jnp.pad(f, 3), stiff_pad, mass_pad, 3, 0), fields)
    first_image = operate_all(panel_in)
    filtered_one = ((first_image - filter_center * panel_in.astype(jnp.float32)) / filter_half).astype(jnp.bfloat16)
    filtered_one = lax.optimization_barrier(filtered_one)
    second_image = operate_all(filtered_one)
    owned_one = filtered_one.astype(jnp.float32)
    filtered = (2.0 * (second_image - filter_center * owned_one) / filter_half - panel_in.astype(jnp.float32)).astype(jnp.bfloat16)
    flat_y = filtered.reshape(VECS, -1)
    flat_p = prior_modes.reshape(PRIOR, -1)
    projections = jnp.dot(flat_p.astype(jnp.float32), flat_y.T.astype(jnp.float32), preferred_element_type=jnp.float32) / NODES
    coeffs = projections.astype(jnp.bfloat16)
    residual = flat_y.astype(jnp.float32) - jnp.dot(coeffs.T.astype(jnp.float32), flat_p.astype(jnp.float32), preferred_element_type=jnp.float32)
    gram_matrix = jnp.dot(residual, residual.T, precision=lax.Precision.HIGHEST) / NODES
    lower_factor = jnp.linalg.cholesky(gram_matrix)
    inverse = jax.scipy.linalg.solve_triangular(lower_factor, jnp.eye(VECS, dtype=jnp.float32), lower=True)
    row_block = jnp.dot(inverse, residual, precision=lax.Precision.HIGHEST)
    return (row_block.reshape(panel_in.shape).astype(jnp.bfloat16), lower_factor.T)
```

```python
import functools

import jax
import jax.numpy as jnp
import ml_dtypes
import numpy as np
from jax import lax
from jax.experimental import pallas as pl
from jax.experimental.pallas import tpu as pltpu
from jax.sharding import PartitionSpec as P

filter_center = 10.0
filter_half = 12.0

MESH = pl.DeviceIdType.MESH
BF16 = jnp.bfloat16
F32 = jnp.float32
VECS = 32
PRIOR = 64
SIDE = 8
ROWS = SIDE * SIDE
LANES = 128
CHUNK = 8
CHUNKS = VECS // CHUNK
PAIRS = CHUNK // 2
SLOT = LANES // CHUNK
POINTS_Z = 5 * (LANES // 4 + 1)


def lobatto_tables():
    points = np.array([-1.0, -np.sqrt(3.0 / 7.0), 0.0, np.sqrt(3.0 / 7.0), 1.0])
    weights = np.array([0.1, 49.0 / 90.0, 32.0 / 45.0, 49.0 / 90.0, 0.1])
    scales = np.array(
        [np.prod([points[i] - points[k] for k in range(5) if k != i]) for i in range(5)]
    )
    derivative = np.zeros((5, 5))
    for i in range(5):
        for j in range(5):
            if j != i:
                derivative[i, j] = scales[i] / scales[j] / (points[i] - points[j])
        derivative[i, i] = -np.sum(derivative[i])
    return (derivative, weights)


def node_weight(count):
    weights = lobatto_tables()[1]
    per_node = [weights[3], weights[4] + weights[0], weights[1], weights[2]]
    return np.array([per_node[i % 4] for i in range(count)])


HIGH_X, HIGH_Y, LOW_X, LOW_Y = 64, 80, 96, 144
BLOCK = 256


def field_row(x, y, parity):
    if x < 0:
        return LOW_X + 24 * parity + (x + 3) * SIDE + y
    if y < 0:
        return LOW_Y + 24 * parity + (y + 3) * SIDE + x
    if x >= SIDE:
        return HIGH_X + (x - SIDE) * SIDE + y
    if y >= SIDE:
        return HIGH_Y + (y - SIDE) * SIDE + x
    return x * SIDE + y


def stiff_row(x, y):
    if x < 0:
        return ROWS + (x + SIDE) * SIDE + y
    if x >= SIDE:
        return 2 * ROWS + (x - SIDE) * SIDE + y
    if y < 0:
        return 3 * ROWS + x * SIDE + y + SIDE
    if y >= SIDE:
        return 4 * ROWS + x * SIDE + y - SIDE
    return x * SIDE + y


STIFF_K = 384


def make_tables():
    derivative, weights = lobatto_tables()
    node_w = node_weight(SIDE)
    node_z = node_weight(LANES)
    grad = np.zeros((2, BLOCK, BLOCK))
    back = np.zeros((ROWS, BLOCK))
    pick = np.zeros((BLOCK, STIFF_K))
    scale = np.zeros((BLOCK, LANES))
    for m in range(3):
        for q in range(5):
            for t in range(SIDE):
                rx = (m * 5 + q) * SIDE + t
                ry = 120 + rx
                at = 4 * m - 3 + q
                pick[rx, stiff_row(at, t)] = 1
                pick[ry, stiff_row(t, at)] = 1
                scale[rx] = weights[q] * node_w[t] * node_z
                scale[ry] = weights[q] * node_w[t] * node_z
                for a in range(5):
                    node = 4 * m - 3 + a
                    for parity in range(2):
                        grad[parity, rx, field_row(node, t, parity)] = derivative[q, a]
                        grad[parity, ry, field_row(t, node, parity)] = derivative[q, a]
                    if 0 <= node < SIDE:
                        back[node * SIDE + t, rx] = derivative[q, a]
                        back[t * SIDE + node, ry] = derivative[q, a]
    grad_z = np.zeros((2 * LANES, BLOCK))
    back_z = np.zeros((BLOCK, LANES))
    pick_z = np.zeros((3 * LANES, BLOCK))
    scale_z = np.zeros((ROWS, BLOCK))
    for m in range(LANES // 4 + 1):
        for q in range(5):
            col = 5 * m + q
            at = 4 * m - 3 + q
            source = at if 0 <= at < LANES else (2 * LANES + at if at < 0 else LANES + at)
            pick_z[source, col] = 1
            for t in range(ROWS):
                scale_z[t, col] = weights[q] * node_w[t // SIDE] * node_w[t % SIDE]
            for a in range(5):
                node = 4 * m - 3 + a
                row = node
                if node < 0:
                    row = LANES + node + 3
                elif node >= LANES:
                    row = LANES + 3 + node - LANES
                else:
                    back_z[col, node] = derivative[q, a]
                grad_z[row, col] = derivative[q, a]
    faces = np.zeros((128, 128))
    for half in range(2):
        for t in range(SIDE):
            for j in range(2):
                faces[16 * half + j * SIDE + t, 64 * half + t * SIDE + j] = 1
            for j in range(3):
                faces[32 + 24 * half + j * SIDE + t, 64 * half + (5 + j) * SIDE + t] = 1
                faces[80 + 24 * half + j * SIDE + t, 64 * half + t * SIDE + 5 + j] = 1
    ends = np.zeros((CHUNK * LANES, LANES))
    for j in range(CHUNK):
        for i in range(5):
            ends[j * LANES + (LANES - 3 + i) % LANES, j * SLOT + i] = 1
    volume = np.zeros((ROWS, LANES))
    for t in range(ROWS):
        volume[t] = node_w[t // SIDE] * node_w[t % SIDE] * node_z
    fold = np.zeros((VECS, VECS * SIDE))
    for v in range(VECS):
        fold[v, v * SIDE : (v + 1) * SIDE] = 1
    spread = np.zeros((2 * VECS * SIDE, 2 * VECS))
    for v in range(2 * VECS):
        spread[v * SIDE : (v + 1) * SIDE, v] = 1
    gather = np.zeros(((VECS + PRIOR) * SIDE, LANES))
    for u in range(VECS + PRIOR):
        gather[u * SIDE : (u + 1) * SIDE, u] = 1
    halves = [grad, back, pick, grad_z, back_z, pick_z, faces, ends, fold, spread, gather]
    singles = [scale, scale_z, volume]
    return [t.astype(np.float32).astype(ml_dtypes.bfloat16) for t in halves] + [
        t.astype(np.float32) for t in singles
    ]


def dot(a, b):
    return jnp.dot(a, b, preferred_element_type=F32)


def dot_nt(a, b, precision=None):
    return lax.dot_general(
        a, b, (((1,), (1,)), ((), ())), precision=precision, preferred_element_type=F32
    )


def split3(a):
    first = a.astype(BF16)
    rest = a - first.astype(F32)
    second = rest.astype(BF16)
    third = (rest - second.astype(F32)).astype(BF16)
    return first, second, third


def side(shape, dim):
    return lax.broadcasted_iota(jnp.int32, shape, dim)


TABLES = 14


def kernel(sizes, nodes_total, *refs):
    panel, prior, stiff, mass = refs[:4]
    tables = refs[4 : 4 + TABLES]
    out, upper = refs[4 + TABLES : 6 + TABLES]
    scratch = refs[6 + TABLES :]
    held = scratch[:TABLES]
    grad, back, pick, grad_z, back_z, pick_z, faces, ends, fold, spread, gather = held[:11]
    scale, scale_z, volume = held[11:]
    (
        field,
        modes,
        stiff_own,
        mass_own,
        once,
        low_x_s,
        high_x_s,
        low_y_s,
        high_y_s,
        ends_s,
        low_x_r,
        high_x_r,
        low_y_r,
        high_y_r,
        low_z_r,
        high_z_r,
        stiff_r,
        factor,
        factor_z,
        shift,
        stack,
        total_s,
        scatter_r,
        sum_x,
        sum_y,
        gathered,
        result,
        load_sem,
        field_sem,
        out_sem,
        stiff_send,
        stiff_recv,
        face_send,
        face_recv,
        sum_send,
        sum_recv,
    ) = scratch[TABLES:]
    nx, ny, nz = sizes
    axes = ("gx", "gy", "gz")
    me = [lax.axis_index(a) for a in axes]

    def along(axis, step):
        return {axes[axis]: lax.rem(me[axis] + step + sizes[axis], sizes[axis])}

    field_loads = []
    for c in range(CHUNKS):
        part = pl.ds(c * CHUNK, CHUNK)
        load = pltpu.make_async_copy(panel.at[part], field.at[part], field_sem.at[c])
        load.start()
        field_loads.append(load)
    loads = []
    for k, (src, dst) in enumerate(
        [(stiff, stiff_own), (mass, mass_own), (prior, modes)] + list(zip(tables, held))
    ):
        load = pltpu.make_async_copy(src, dst, load_sem.at[k])
        load.start()
        loads.append(load)
    barrier = pltpu.get_barrier_semaphore()
    for axis in range(3):
        for step in range(1, sizes[axis]):
            pl.semaphore_signal(
                barrier, inc=1, device_id=along(axis, step), device_id_type=MESH
            )

    def pack(app, c, source):
        cells = [source[c * CHUNK + j] for j in range(CHUNK)]
        pairs = [
            jnp.concatenate([cells[2 * p], cells[2 * p + 1]], axis=1) for p in range(PAIRS)
        ]
        for p in range(PAIRS):
            high_x_s[app, c, 16 * p : 16 * p + 16] = pairs[p][:16]
        for q in range(PAIRS // 2):
            both = jnp.concatenate([pairs[2 * q], pairs[2 * q + 1]], axis=0)
            picked = dot(faces[...], both).astype(BF16)
            high_y_s[app, c, 32 * q : 32 * q + 32] = picked[:32]
            low_x_s[app, c, 48 * q : 48 * q + 48] = picked[32:80]
            low_y_s[app, c, 48 * q : 48 * q + 48] = picked[80:]
        ends_s[app, c] = dot(jnp.concatenate(cells, axis=1), ends[...]).astype(BF16)

    def face_copies(app, c):
        plan = [
            (low_x_s, low_x_r, 0, 1),
            (high_x_s, high_x_r, 0, -1),
            (low_y_s, low_y_r, 1, 1),
            (high_y_s, high_y_r, 1, -1),
            (ends_s, low_z_r, 2, 1),
            (ends_s, high_z_r, 2, -1),
        ]
        return [
            pltpu.make_async_remote_copy(
                src_ref=src.at[app, c],
                dst_ref=dst.at[app, c],
                send_sem=face_send.at[app, c, k],
                recv_sem=face_recv.at[app, c, k],
                device_id=along(axis, step),
                device_id_type=MESH,
            )
            for k, (src, dst, axis, step) in enumerate(plan)
        ]

    def stiff_copies():
        return [
            pltpu.make_async_remote_copy(
                src_ref=stiff_own,
                dst_ref=stiff_r.at[k],
                send_sem=stiff_send.at[k],
                recv_sem=stiff_recv.at[k],
                device_id=along(k // 2, 1 - 2 * (k % 2)),
                device_id_type=MESH,
            )
            for k in range(6)
        ]

    for load in loads:
        load.wait()
    for load in field_loads:
        load.wait()

    @pl.loop(0, CHUNKS)
    def _(c):
        pack(0, c, field)

    pl.semaphore_wait(barrier, nx + ny + nz - 3)
    for copy in stiff_copies():
        copy.start()

    @pl.loop(0, CHUNKS)
    def _(c):
        for copy in face_copies(0, c):
            copy.start()

    first = [me[k] == 0 for k in range(3)]
    last = [me[k] == sizes[k] - 1 for k in range(3)]

    def outside(index, spans):
        cut = index < 0
        for low, high, missing in spans:
            cut = cut | ((index >= low) & (index < high) & missing)
        return cut

    col = side((BLOCK, BLOCK), 1)
    cut = outside(
        col,
        [
            (HIGH_X, HIGH_Y, last[0]),
            (HIGH_Y, LOW_X, last[1]),
            (LOW_X, LOW_Y, first[0]),
            (LOW_Y, LOW_Y + 48, first[1]),
        ],
    )
    for parity in range(2):
        grad[parity] = jnp.where(cut, 0.0, grad[parity].astype(F32)).astype(BF16)
    row = side((2 * LANES, BLOCK), 0)
    cut = outside(row, [(LANES, LANES + 3, first[2]), (LANES + 3, LANES + 5, last[2])])
    grad_z[...] = jnp.where(cut, 0.0, grad_z[...].astype(F32)).astype(BF16)
    col = side((BLOCK, STIFF_K), 1)
    cut = outside(
        col,
        [
            (ROWS, 2 * ROWS, first[0]),
            (2 * ROWS, 3 * ROWS, last[0]),
            (3 * ROWS, 4 * ROWS, first[1]),
            (4 * ROWS, 5 * ROWS, last[1]),
        ],
    )
    pick[...] = jnp.where(cut, 0.0, pick[...].astype(F32)).astype(BF16)
    row = side((3 * LANES, BLOCK), 0)
    cut = outside(row, [(LANES, 2 * LANES, first[2]), (2 * LANES, 3 * LANES, last[2])])
    pick_z[...] = jnp.where(cut, 0.0, pick_z[...].astype(F32)).astype(BF16)

    shift[...] = volume[...] * mass_own[...].astype(F32) + filter_center

    @pl.loop(0, PRIOR // 2)
    def _(p):
        one = modes[2 * p].astype(F32)
        two = modes[2 * p + 1].astype(F32)
        at = pl.ds(pl.multiple_of(VECS * SIDE + 16 * p, 16), 16)
        for x in range(SIDE):
            rows = slice(x * SIDE, (x + 1) * SIDE)
            stack[at, x * LANES : (x + 1) * LANES] = jnp.concatenate(
                [one[rows], two[rows]], axis=0
            ).astype(BF16)

    for copy in stiff_copies():
        copy.wait_recv()
    around = jnp.concatenate(
        [stiff_own[...]]
        + [stiff_r[k] for k in range(4)]
        + [jnp.zeros((STIFF_K - 5 * ROWS, LANES), BF16)],
        axis=0,
    )
    factor[...] = dot(pick[...], around) * scale[...]
    around = jnp.concatenate([stiff_own[...], stiff_r[4], stiff_r[5]], axis=1)
    factor_z[...] = dot(around, pick_z[...]) * scale_z[...]

    def operate(app, c, source, finish):
        slot = lax.rem(side((ROWS, LANES), 1), SLOT)
        joined = jnp.where(
            slot < 3, low_z_r[app, c].astype(F32), high_z_r[app, c].astype(F32)
        )
        factor_two = jnp.concatenate([factor[...], factor[...]], axis=1)
        factor_rows = jnp.concatenate([factor_z[...], factor_z[...]], axis=0)
        for p in range(PAIRS):
            q, parity = p // 2, p % 2
            cells = [source[c * CHUNK + 2 * p + h] for h in range(2)]
            rows = jnp.concatenate(
                [
                    jnp.concatenate(cells, axis=1),
                    high_x_r[app, c, 16 * p : 16 * p + 16],
                    high_y_r[app, c, 16 * p : 16 * p + 16],
                    low_x_r[app, c, 48 * q : 48 * q + 48],
                    low_y_r[app, c, 48 * q : 48 * q + 48],
                    jnp.zeros((BLOCK - 192, 2 * LANES), BF16),
                ],
                axis=0,
            )
            flux = (dot(grad[parity], rows) * factor_two).astype(BF16)
            image = dot(back[...], flux)
            lines = []
            for h in range(2):
                j = 2 * p + h
                rolled = pltpu.roll(joined, LANES - SLOT * j, 1) if j else joined
                lines.append(jnp.concatenate([cells[h], rolled.astype(BF16)], axis=1))
            flux_z = (dot(jnp.concatenate(lines, axis=0), grad_z[...]) * factor_rows).astype(
                BF16
            )
            image_z = dot(flux_z, back_z[...])
            moved = [
                image[:, h * LANES : (h + 1) * LANES]
                + image_z[h * ROWS : (h + 1) * ROWS]
                - shift[...] * cells[h].astype(F32)
                for h in range(2)
            ]
            finish(c, p, moved)

    def finish_one(c, p, moved):
        for h in range(2):
            once[c * CHUNK + 2 * p + h] = (moved[h] * (1.0 / filter_half)).astype(BF16)

    def finish_two(c, p, moved):
        done = [
            moved[h] * (2.0 / filter_half) - field[c * CHUNK + 2 * p + h].astype(F32)
            for h in range(2)
        ]
        at = pl.ds(pl.multiple_of(c * (CHUNK * SIDE) + 16 * p, 16), 16)
        for x in range(SIDE):
            rows = slice(x * SIDE, (x + 1) * SIDE)
            stack[at, x * LANES : (x + 1) * LANES] = jnp.concatenate(
                [done[0][rows], done[1][rows]], axis=0
            ).astype(BF16)

    @pl.loop(0, CHUNKS)
    def _(c):
        for copy in face_copies(0, c):
            copy.wait_recv()
        operate(0, c, field, finish_one)
        pack(1, c, once)
        for copy in face_copies(1, c):
            copy.start()

    @pl.loop(0, CHUNKS)
    def _(c):
        for copy in face_copies(1, c):
            copy.wait_recv()
        operate(1, c, once, finish_two)

    wide = VECS * SIDE
    tall = (VECS + PRIOR) * SIDE
    cross = dot_nt(stack[:wide], stack[...])
    same = lax.rem(side((wide, tall), 0), SIDE) == lax.rem(side((wide, tall), 1), SIDE)
    folded = sum(dot(fold[...], t) for t in split3(jnp.where(same, cross, 0.0)))
    sums = sum(dot(t, gather[...]) for t in split3(folded))

    share = VECS // nz

    def sum_copies(stage, axis, source, target):
        copies = []
        for step in range(1, sizes[axis]):
            to = lax.rem(me[axis] + step, sizes[axis])
            copies.append(
                pltpu.make_async_remote_copy(
                    src_ref=source(to),
                    dst_ref=target(step),
                    send_sem=sum_send.at[stage, step],
                    recv_sem=sum_recv.at[stage, step],
                    device_id={axes[axis]: to},
                    device_id_type=MESH,
                )
            )
        for copy in copies:
            copy.start()
        for copy in copies:
            copy.wait_recv()
        return copies

    for k in range(nz):
        total_s[k] = sums[k * share : (k + 1) * share]
    sent = sum_copies(0, 2, lambda to: total_s.at[to], lambda step: scatter_r.at[step])
    mine = total_s[me[2]]
    for step in range(1, nz):
        mine = mine + scatter_r[step]
    for stage, axis, slots in ((1, 0, sum_x), (2, 1, sum_y)):
        slots[me[axis]] = mine
        here = slots.at[me[axis]]
        sent += sum_copies(stage, axis, lambda to: here, lambda step: here)
        mine = slots[0]
        for k in range(1, sizes[axis]):
            mine = mine + slots[k]
    gathered[me[2]] = mine
    here = gathered.at[me[2]]
    sent += sum_copies(3, 2, lambda to: here, lambda step: here)
    sums = jnp.concatenate([gathered[k] for k in range(nz)], axis=0) * (1.0 / nodes_total)

    lane = side((VECS, LANES), 1)
    line = side((VECS, LANES), 0)
    proj = jnp.where((lane >= VECS) & (lane < VECS + PRIOR), sums, 0.0)
    coeffs = proj.astype(BF16).astype(F32)
    rest = proj - coeffs
    exact = lax.Precision.HIGHEST
    gram = sums[:, :VECS] - dot_nt(proj, proj, exact) + dot_nt(rest, rest, exact)
    solve = jnp.where(lane == line, 1.0, 0.0) - coeffs
    below = side((VECS, 1), 0)
    for k in range(VECS):
        ratio = jnp.where(below > k, gram[:, k : k + 1] / gram[k : k + 1, k : k + 1], 0.0)
        solve = solve - ratio * solve[k : k + 1]
        gram = gram - ratio * gram[k : k + 1]
    left = side((VECS, VECS), 0)
    right = side((VECS, VECS), 1)
    pivots = jnp.sum(jnp.where(left == right, gram, 0.0), axis=1, keepdims=True)
    inverse = 1.0 / jnp.sqrt(pivots)
    upper[...] = jnp.where(right >= left, gram * inverse, 0.0)
    solve = solve * inverse

    high = solve.astype(BF16)
    low = (solve - high.astype(F32)).astype(BF16)
    widened = dot_nt(jnp.concatenate([high, low], axis=0), gather[...]).astype(BF16)
    widened = dot(spread[...], widened)
    shape = (2 * wide, tall)
    same = lax.rem(side(shape, 0), SIDE) == lax.rem(side(shape, 1), SIDE)
    widened = jnp.where(same, widened, 0.0).astype(BF16)
    writes = []
    for x in range(0, SIDE, 2):
        block = dot(widened, stack[:, x * LANES : (x + 2) * LANES])
        block = block[:wide] + block[wide:]
        for v in range(VECS):
            rows = block[v * SIDE : (v + 1) * SIDE]
            result[v, x * SIDE : (x + 2) * SIDE] = jnp.concatenate(
                [rows[:, :LANES], rows[:, LANES:]], axis=0
            ).astype(BF16)
        part = pl.ds(x * SIDE, 2 * SIDE)
        write = pltpu.make_async_copy(
            result.at[:, part], out.at[:, part], out_sem.at[x // 2]
        )
        write.start()
        writes.append(write)

    for copy in sent + stiff_copies():
        copy.wait_send()

    @pl.loop(0, CHUNKS)
    def _(c):
        for app in range(2):
            for copy in face_copies(app, c):
                copy.wait_send()

    for write in writes:
        write.wait()


def on_device(sizes, nodes_total, panel_in, prior_modes, stiffness, mass_shift):
    nx, ny, nz = sizes
    share = VECS // nz
    tables = make_tables()
    low = (2, CHUNKS, 24 * PAIRS, 2 * LANES)
    high = (2, CHUNKS, 16 * PAIRS, 2 * LANES)
    flat = (2, CHUNKS, ROWS, LANES)
    any_space = pl.BlockSpec(memory_space=pl.ANY)
    dma = pltpu.SemaphoreType.DMA
    basis, upper = pl.pallas_call(
        functools.partial(kernel, sizes, nodes_total),
        out_shape=(
            jax.ShapeDtypeStruct((VECS, ROWS, LANES), BF16),
            jax.ShapeDtypeStruct((VECS, VECS), F32),
        ),
        in_specs=[any_space] * (4 + TABLES),
        out_specs=(any_space, pl.BlockSpec(memory_space=pltpu.VMEM)),
        scratch_shapes=[pltpu.VMEM(t.shape, t.dtype) for t in tables]
        + [
            pltpu.VMEM((VECS, ROWS, LANES), BF16),
            pltpu.VMEM((PRIOR, ROWS, LANES), BF16),
            pltpu.VMEM((ROWS, LANES), BF16),
            pltpu.VMEM((ROWS, LANES), BF16),
            pltpu.VMEM((VECS, ROWS, LANES), BF16),
            pltpu.VMEM(low, BF16),
            pltpu.VMEM(high, BF16),
            pltpu.VMEM(low, BF16),
            pltpu.VMEM(high, BF16),
            pltpu.VMEM(flat, BF16),
            pltpu.VMEM(low, BF16),
            pltpu.VMEM(high, BF16),
            pltpu.VMEM(low, BF16),
            pltpu.VMEM(high, BF16),
            pltpu.VMEM(flat, BF16),
            pltpu.VMEM(flat, BF16),
            pltpu.VMEM((6, ROWS, LANES), BF16),
            pltpu.VMEM((BLOCK, LANES), F32),
            pltpu.VMEM((ROWS, BLOCK), F32),
            pltpu.VMEM((ROWS, LANES), F32),
            pltpu.VMEM(((VECS + PRIOR) * SIDE, SIDE * LANES), BF16),
            pltpu.VMEM((nz, share, LANES), F32),
            pltpu.VMEM((nz, share, LANES), F32),
            pltpu.VMEM((nx, share, LANES), F32),
            pltpu.VMEM((ny, share, LANES), F32),
            pltpu.VMEM((nz, share, LANES), F32),
            pltpu.VMEM((VECS, ROWS, LANES), BF16),
            dma((3 + TABLES,)),
            dma((CHUNKS,)),
            dma((SIDE // 2,)),
            dma((6,)),
            dma((6,)),
            dma((2, CHUNKS, 6)),
            dma((2, CHUNKS, 6)),
            dma((4, max(sizes))),
            dma((4, max(sizes))),
        ],
        compiler_params=pltpu.CompilerParams(
            collective_id=0, has_side_effects=True, vmem_limit_bytes=56 * 2**20
        ),
    )(
        panel_in.reshape(VECS, ROWS, LANES),
        prior_modes.reshape(PRIOR, ROWS, LANES),
        stiffness.reshape(ROWS, LANES),
        mass_shift.reshape(ROWS, LANES),
        *[jnp.asarray(t) for t in tables],
    )
    return basis.reshape(panel_in.shape), upper


def solution(mesh):
    sizes = tuple(mesh.shape[a] for a in ("gx", "gy", "gz"))
    nodes_total = ROWS * LANES * sizes[0] * sizes[1] * sizes[2]
    placed = (
        P(None, "gx", "gy", "gz"),
        P(None, "gx", "gy", "gz"),
        P("gx", "gy", "gz"),
        P("gx", "gy", "gz"),
    )
    return jax.shard_map(
        functools.partial(on_device, sizes, nodes_total),
        mesh=mesh,
        in_specs=placed,
        out_specs=(P(None, "gx", "gy", "gz"), P()),
        check_vma=False,
    )
```

```python
import functools

import jax
import jax.numpy as jnp
import ml_dtypes
import numpy as np
from jax import lax
from jax.experimental import pallas as pl
from jax.experimental.pallas import tpu as pltpu
from jax.sharding import PartitionSpec as P

filter_center = 10.0
filter_half = 12.0

MESH = pl.DeviceIdType.MESH
BF16 = jnp.bfloat16
F32 = jnp.float32
VECS = 32
PRIOR = 64
SIDE = 8
ROWS = SIDE * SIDE
LANES = 128
CHUNK = 8
CHUNKS = VECS // CHUNK
PAIRS = CHUNK // 2
SLOT = LANES // CHUNK
POINTS_Z = 5 * (LANES // 4 + 1)


def lobatto_tables():
    points = np.array([-1.0, -np.sqrt(3.0 / 7.0), 0.0, np.sqrt(3.0 / 7.0), 1.0])
    weights = np.array([0.1, 49.0 / 90.0, 32.0 / 45.0, 49.0 / 90.0, 0.1])
    scales = np.array(
        [np.prod([points[i] - points[k] for k in range(5) if k != i]) for i in range(5)]
    )
    derivative = np.zeros((5, 5))
    for i in range(5):
        for j in range(5):
            if j != i:
                derivative[i, j] = scales[i] / scales[j] / (points[i] - points[j])
        derivative[i, i] = -np.sum(derivative[i])
    return (derivative, weights)


def node_weight(count):
    weights = lobatto_tables()[1]
    per_node = [weights[3], weights[4] + weights[0], weights[1], weights[2]]
    return np.array([per_node[i % 4] for i in range(count)])


HIGH_X, HIGH_Y, LOW_X, LOW_Y = 64, 80, 96, 144
BLOCK = 256


def field_row(x, y, parity):
    if x < 0:
        return LOW_X + 24 * parity + (x + 3) * SIDE + y
    if y < 0:
        return LOW_Y + 24 * parity + (y + 3) * SIDE + x
    if x >= SIDE:
        return HIGH_X + (x - SIDE) * SIDE + y
    if y >= SIDE:
        return HIGH_Y + (y - SIDE) * SIDE + x
    return x * SIDE + y


def stiff_row(x, y):
    if x < 0:
        return ROWS + (x + SIDE) * SIDE + y
    if x >= SIDE:
        return 2 * ROWS + (x - SIDE) * SIDE + y
    if y < 0:
        return 3 * ROWS + x * SIDE + y + SIDE
    if y >= SIDE:
        return 4 * ROWS + x * SIDE + y - SIDE
    return x * SIDE + y


STIFF_K = 384


def make_tables():
    derivative, weights = lobatto_tables()
    node_w = node_weight(SIDE)
    node_z = node_weight(LANES)
    grad = np.zeros((2, BLOCK, BLOCK))
    back = np.zeros((ROWS, BLOCK))
    pick = np.zeros((BLOCK, STIFF_K))
    scale = np.zeros((BLOCK, LANES))
    for m in range(3):
        for q in range(5):
            for t in range(SIDE):
                rx = (m * 5 + q) * SIDE + t
                ry = 120 + rx
                at = 4 * m - 3 + q
                pick[rx, stiff_row(at, t)] = 1
                pick[ry, stiff_row(t, at)] = 1
                scale[rx] = weights[q] * node_w[t] * node_z
                scale[ry] = weights[q] * node_w[t] * node_z
                for a in range(5):
                    node = 4 * m - 3 + a
                    for parity in range(2):
                        grad[parity, rx, field_row(node, t, parity)] = derivative[q, a]
                        grad[parity, ry, field_row(t, node, parity)] = derivative[q, a]
                    if 0 <= node < SIDE:
                        back[node * SIDE + t, rx] = derivative[q, a]
                        back[t * SIDE + node, ry] = derivative[q, a]
    grad_z = np.zeros((2 * LANES, BLOCK))
    back_z = np.zeros((BLOCK, LANES))
    pick_z = np.zeros((3 * LANES, BLOCK))
    scale_z = np.zeros((ROWS, BLOCK))
    for m in range(LANES // 4 + 1):
        for q in range(5):
            col = 5 * m + q
            at = 4 * m - 3 + q
            source = at if 0 <= at < LANES else (2 * LANES + at if at < 0 else LANES + at)
            pick_z[source, col] = 1
            for t in range(ROWS):
                scale_z[t, col] = weights[q] * node_w[t // SIDE] * node_w[t % SIDE]
            for a in range(5):
                node = 4 * m - 3 + a
                row = node
                if node < 0:
                    row = LANES + node + 3
                elif node >= LANES:
                    row = LANES + 3 + node - LANES
                else:
                    back_z[col, node] = derivative[q, a]
                grad_z[row, col] = derivative[q, a]
    faces = np.zeros((128, 128))
    for half in range(2):
        for t in range(SIDE):
            for j in range(2):
                faces[16 * half + j * SIDE + t, 64 * half + t * SIDE + j] = 1
            for j in range(3):
                faces[32 + 24 * half + j * SIDE + t, 64 * half + (5 + j) * SIDE + t] = 1
                faces[80 + 24 * half + j * SIDE + t, 64 * half + t * SIDE + 5 + j] = 1
    ends = np.zeros((CHUNK * LANES, LANES))
    for j in range(CHUNK):
        for i in range(5):
            ends[j * LANES + (LANES - 3 + i) % LANES, j * SLOT + i] = 1
    volume = np.zeros((ROWS, LANES))
    for t in range(ROWS):
        volume[t] = node_w[t // SIDE] * node_w[t % SIDE] * node_z
    fold = np.zeros((VECS, VECS * SIDE))
    for v in range(VECS):
        fold[v, v * SIDE : (v + 1) * SIDE] = 1
    spread = np.zeros((2 * VECS * SIDE, 2 * VECS))
    for v in range(2 * VECS):
        spread[v * SIDE : (v + 1) * SIDE, v] = 1
    gather = np.zeros(((VECS + PRIOR) * SIDE, LANES))
    for u in range(VECS + PRIOR):
        gather[u * SIDE : (u + 1) * SIDE, u] = 1
    halves = [grad, back, pick, grad_z, back_z, pick_z, faces, ends, fold, spread, gather]
    singles = [scale, scale_z, volume]
    return [t.astype(np.float32).astype(ml_dtypes.bfloat16) for t in halves] + [
        t.astype(np.float32) for t in singles
    ]


def dot(a, b):
    return jnp.dot(a, b, preferred_element_type=F32)


def dot_nt(a, b, precision=None):
    return lax.dot_general(
        a, b, (((1,), (1,)), ((), ())), precision=precision, preferred_element_type=F32
    )


def split3(a):
    first = a.astype(BF16)
    rest = a - first.astype(F32)
    second = rest.astype(BF16)
    third = (rest - second.astype(F32)).astype(BF16)
    return first, second, third


def side(shape, dim):
    return lax.broadcasted_iota(jnp.int32, shape, dim)


TABLES = 14


def kernel(sizes, nodes_total, *refs):
    panel, prior, stiff, mass = refs[:4]
    tables = refs[4 : 4 + TABLES]
    out, upper = refs[4 + TABLES : 6 + TABLES]
    scratch = refs[6 + TABLES :]
    held = scratch[:TABLES]
    grad, back, pick, grad_z, back_z, pick_z, faces, ends, fold, spread, gather = held[:11]
    scale, scale_z, volume = held[11:]
    (
        field,
        modes,
        stiff_own,
        mass_own,
        once,
        low_x_s,
        high_x_s,
        low_y_s,
        high_y_s,
        ends_s,
        low_x_r,
        high_x_r,
        low_y_r,
        high_y_r,
        low_z_r,
        high_z_r,
        stiff_r,
        factor,
        factor_z,
        shift,
        stack,
        flux,
        flux_z,
        slots_z,
        slots_x,
        slots_y,
        result,
        load_sem,
        out_sem,
        stiff_send,
        stiff_recv,
        face_send,
        face_recv,
        sum_send,
        sum_recv,
    ) = scratch[TABLES:]
    nx, ny, nz = sizes
    axes = ("gx", "gy", "gz")
    me = [lax.axis_index(a) for a in axes]

    def along(axis, step):
        return {axes[axis]: lax.rem(me[axis] + step + sizes[axis], sizes[axis])}

    barrier = pltpu.get_barrier_semaphore()
    for axis in range(3):
        for step in range(1, sizes[axis]):
            pl.semaphore_signal(
                barrier, inc=1, device_id=along(axis, step), device_id_type=MESH
            )
    loads = {}

    def load(name, src, dst):
        loads[name] = pltpu.make_async_copy(src, dst, load_sem.at[len(loads)])
        loads[name].start()

    def loaded(*names):
        for name in names:
            loads[name].wait()

    load("faces", tables[6], faces)
    for c in range(CHUNKS):
        part = pl.ds(c * CHUNK, CHUNK)
        load(c, panel.at[part], field.at[part])
    load("ends", tables[7], ends)
    load("stiff", stiff, stiff_own)

    def pack(app, c, source):
        cells = [source[c * CHUNK + j] for j in range(CHUNK)]
        pairs = [
            jnp.concatenate([cells[2 * p], cells[2 * p + 1]], axis=1) for p in range(PAIRS)
        ]
        for p in range(PAIRS):
            high_x_s[app, c, 16 * p : 16 * p + 16] = pairs[p][:16]
        for q in range(PAIRS // 2):
            both = jnp.concatenate([pairs[2 * q], pairs[2 * q + 1]], axis=0)
            picked = dot(faces[...], both).astype(BF16)
            high_y_s[app, c, 32 * q : 32 * q + 32] = picked[:32]
            low_x_s[app, c, 48 * q : 48 * q + 48] = picked[32:80]
            low_y_s[app, c, 48 * q : 48 * q + 48] = picked[80:]
        ends_s[app, c] = dot(jnp.concatenate(cells, axis=1), ends[...]).astype(BF16)

    def face_copies(app, c):
        plan = [
            (low_x_s, low_x_r, 0, 1),
            (high_x_s, high_x_r, 0, -1),
            (low_y_s, low_y_r, 1, 1),
            (high_y_s, high_y_r, 1, -1),
            (ends_s, low_z_r, 2, 1),
            (ends_s, high_z_r, 2, -1),
        ]
        return [
            pltpu.make_async_remote_copy(
                src_ref=src.at[app, c],
                dst_ref=dst.at[app, c],
                send_sem=face_send.at[app, c, k],
                recv_sem=face_recv.at[app, c, k],
                device_id=along(axis, step),
                device_id_type=MESH,
            )
            for k, (src, dst, axis, step) in enumerate(plan)
        ]

    def stiff_copies():
        return [
            pltpu.make_async_remote_copy(
                src_ref=stiff_own,
                dst_ref=stiff_r.at[k],
                send_sem=stiff_send.at[k],
                recv_sem=stiff_recv.at[k],
                device_id=along(k // 2, 1 - 2 * (k % 2)),
                device_id_type=MESH,
            )
            for k in range(6)
        ]

    loaded("faces", "ends")
    for c in range(CHUNKS):
        loaded(c)
        pack(0, c, field)
    for k in (0, 2, 3, 5, 11, 12, 13, 1, 4):
        load("table%d" % k, tables[k], held[k])
    load("mass", mass, mass_own)
    load("prior", prior, modes)
    for k in (8, 9, 10):
        load("table%d" % k, tables[k], held[k])
    loaded("stiff")
    pl.semaphore_wait(barrier, nx + ny + nz - 3)
    for copy in stiff_copies():
        copy.start()

    @pl.loop(0, CHUNKS)
    def _(c):
        for copy in face_copies(0, c):
            copy.start()

    loaded("table0", "table2", "table3", "table5")

    first = [me[k] == 0 for k in range(3)]
    last = [me[k] == sizes[k] - 1 for k in range(3)]

    def outside(index, spans):
        cut = index < 0
        for low, high, missing in spans:
            cut = cut | ((index >= low) & (index < high) & missing)
        return cut

    col = side((BLOCK, BLOCK), 1)
    cut = outside(
        col,
        [
            (HIGH_X, HIGH_Y, last[0]),
            (HIGH_Y, LOW_X, last[1]),
            (LOW_X, LOW_Y, first[0]),
            (LOW_Y, LOW_Y + 48, first[1]),
        ],
    )
    for parity in range(2):
        grad[parity] = jnp.where(cut, 0.0, grad[parity].astype(F32)).astype(BF16)
    row = side((2 * LANES, BLOCK), 0)
    cut = outside(row, [(LANES, LANES + 3, first[2]), (LANES + 3, LANES + 5, last[2])])
    grad_z[...] = jnp.where(cut, 0.0, grad_z[...].astype(F32)).astype(BF16)
    col = side((BLOCK, STIFF_K), 1)
    cut = outside(
        col,
        [
            (ROWS, 2 * ROWS, first[0]),
            (2 * ROWS, 3 * ROWS, last[0]),
            (3 * ROWS, 4 * ROWS, first[1]),
            (4 * ROWS, 5 * ROWS, last[1]),
        ],
    )
    pick[...] = jnp.where(cut, 0.0, pick[...].astype(F32)).astype(BF16)
    row = side((3 * LANES, BLOCK), 0)
    cut = outside(row, [(LANES, 2 * LANES, first[2]), (2 * LANES, 3 * LANES, last[2])])
    pick_z[...] = jnp.where(cut, 0.0, pick_z[...].astype(F32)).astype(BF16)

    loaded("table11", "table12", "table13", "mass")
    shift[...] = volume[...] * mass_own[...].astype(F32) + filter_center

    loaded("table1", "table4", "table8", "table9", "table10", "prior")

    @pl.loop(0, PRIOR // 2)
    def _(p):
        one = modes[2 * p].astype(F32)
        two = modes[2 * p + 1].astype(F32)
        at = pl.ds(pl.multiple_of(VECS * SIDE + 16 * p, 16), 16)
        for x in range(SIDE):
            rows = slice(x * SIDE, (x + 1) * SIDE)
            stack[at, x * LANES : (x + 1) * LANES] = jnp.concatenate(
                [one[rows], two[rows]], axis=0
            ).astype(BF16)

    for copy in stiff_copies():
        copy.wait_recv()
    around = jnp.concatenate(
        [stiff_own[...]]
        + [stiff_r[k] for k in range(4)]
        + [jnp.zeros((STIFF_K - 5 * ROWS, LANES), BF16)],
        axis=0,
    )
    factor[...] = dot(pick[...], around) * scale[...]
    around = jnp.concatenate([stiff_own[...], stiff_r[4], stiff_r[5]], axis=1)
    factor_z[...] = dot(around, pick_z[...]) * scale_z[...]

    def operate(app, c, source, finish):
        slot = lax.rem(side((ROWS, LANES), 1), SLOT)
        joined = jnp.where(
            slot < 3, low_z_r[app, c].astype(F32), high_z_r[app, c].astype(F32)
        )
        cells = [source[c * CHUNK + j] for j in range(CHUNK)]
        lines = []
        for j in range(CHUNK):
            rolled = pltpu.roll(joined, LANES - SLOT * j, 1) if j else joined
            lines.append(jnp.concatenate([cells[j], rolled.astype(BF16)], axis=1))
        factor_rows = jnp.concatenate([factor_z[...]] * CHUNK, axis=0)
        flux_z[...] = (
            dot(jnp.concatenate(lines, axis=0), grad_z[...]) * factor_rows
        ).astype(BF16)
        factor_two = jnp.concatenate([factor[...], factor[...]], axis=1)
        for p in range(PAIRS):
            q, parity = p // 2, p % 2
            rows = jnp.concatenate(
                [
                    jnp.concatenate(cells[2 * p : 2 * p + 2], axis=1),
                    high_x_r[app, c, 16 * p : 16 * p + 16],
                    high_y_r[app, c, 16 * p : 16 * p + 16],
                    low_x_r[app, c, 48 * q : 48 * q + 48],
                    low_y_r[app, c, 48 * q : 48 * q + 48],
                    jnp.zeros((BLOCK - 192, 2 * LANES), BF16),
                ],
                axis=0,
            )
            flux[p] = (dot(grad[parity], rows) * factor_two).astype(BF16)
        image_z = dot(flux_z[...], back_z[...])
        for p in range(PAIRS):
            image = dot(back[...], flux[p])
            moved = [
                image[:, h * LANES : (h + 1) * LANES]
                + image_z[(2 * p + h) * ROWS : (2 * p + h + 1) * ROWS]
                - shift[...] * cells[2 * p + h].astype(F32)
                for h in range(2)
            ]
            finish(c, p, moved)

    def finish_one(c, p, moved):
        for h in range(2):
            once[c * CHUNK + 2 * p + h] = (moved[h] * (1.0 / filter_half)).astype(BF16)

    def finish_two(c, p, moved):
        done = [
            moved[h] * (2.0 / filter_half) - field[c * CHUNK + 2 * p + h].astype(F32)
            for h in range(2)
        ]
        at = pl.ds(pl.multiple_of(c * (CHUNK * SIDE) + 16 * p, 16), 16)
        for x in range(SIDE):
            rows = slice(x * SIDE, (x + 1) * SIDE)
            stack[at, x * LANES : (x + 1) * LANES] = jnp.concatenate(
                [done[0][rows], done[1][rows]], axis=0
            ).astype(BF16)

    @pl.loop(0, CHUNKS)
    def _(c):
        for copy in face_copies(0, c):
            copy.wait_recv()
        operate(0, c, field, finish_one)
        pack(1, c, once)
        for copy in face_copies(1, c):
            copy.start()

    @pl.loop(0, CHUNKS)
    def _(c):
        for copy in face_copies(1, c):
            copy.wait_recv()
        operate(1, c, once, finish_two)

    wide = VECS * SIDE
    tall = (VECS + PRIOR) * SIDE
    cross = dot_nt(stack[:wide], stack[...])
    same = lax.rem(side((wide, tall), 0), SIDE) == lax.rem(side((wide, tall), 1), SIDE)
    folded = sum(dot(fold[...], t) for t in split3(jnp.where(same, cross, 0.0)))
    sums = sum(dot(t, gather[...]) for t in split3(folded))

    lane = side((8, LANES), 1)
    used = VECS + PRIOR
    tail = sums[24:]
    mine = jnp.concatenate(
        [
            jnp.where(lane < used, sums[8 * r : 8 * r + 8], pltpu.roll(tail, used - 32 * r, 1))
            for r in range(3)
        ],
        axis=0,
    )
    sent = []
    for stage, (axis, slots) in enumerate(((2, slots_z), (0, slots_x), (1, slots_y))):
        slots[me[axis]] = mine
        here = slots.at[me[axis]]
        copies = [
            pltpu.make_async_remote_copy(
                src_ref=here,
                dst_ref=here,
                send_sem=sum_send.at[stage, step],
                recv_sem=sum_recv.at[stage, step],
                device_id=along(axis, step),
                device_id_type=MESH,
            )
            for step in range(1, sizes[axis])
        ]
        for copy in copies:
            copy.start()
        for copy in copies:
            copy.wait_recv()
        sent += copies
        mine = slots[0]
        for k in range(1, sizes[axis]):
            mine = mine + slots[k]
    tail = jnp.zeros((8, LANES), F32)
    for r in range(3):
        part = pltpu.roll(mine[8 * r : 8 * r + 8], LANES - used + 32 * r, 1)
        tail = jnp.where((lane >= 32 * r) & (lane < 32 * r + 32), part, tail)
    sums = jnp.concatenate([mine, tail], axis=0) * (1.0 / nodes_total)

    lane = side((VECS, LANES), 1)
    line = side((VECS, LANES), 0)
    proj = jnp.where((lane >= VECS) & (lane < VECS + PRIOR), sums, 0.0)
    coeffs = proj.astype(BF16).astype(F32)
    rest = proj - coeffs
    exact = lax.Precision.HIGHEST
    gram = sums[:, :VECS] - dot_nt(proj, proj, exact) + dot_nt(rest, rest, exact)
    solve = jnp.where(lane == line, 1.0, 0.0) - coeffs
    below = side((VECS, 1), 0)
    for k in range(VECS):
        ratio = jnp.where(below > k, gram[:, k : k + 1] / gram[k : k + 1, k : k + 1], 0.0)
        solve = solve - ratio * solve[k : k + 1]
        gram = gram - ratio * gram[k : k + 1]
    left = side((VECS, VECS), 0)
    right = side((VECS, VECS), 1)
    pivots = jnp.sum(jnp.where(left == right, gram, 0.0), axis=1, keepdims=True)
    inverse = 1.0 / jnp.sqrt(pivots)
    upper[...] = jnp.where(right >= left, gram * inverse, 0.0)
    solve = solve * inverse

    high = solve.astype(BF16)
    low = (solve - high.astype(F32)).astype(BF16)
    widened = dot_nt(jnp.concatenate([high, low], axis=0), gather[...]).astype(BF16)
    widened = dot(spread[...], widened)
    shape = (2 * wide, tall)
    same = lax.rem(side(shape, 0), SIDE) == lax.rem(side(shape, 1), SIDE)
    widened = jnp.where(same, widened, 0.0).astype(BF16)
    writes = []
    for x in range(0, SIDE, 2):
        block = dot(widened, stack[:, x * LANES : (x + 2) * LANES])
        block = block[:wide] + block[wide:]
        for v in range(VECS):
            rows = block[v * SIDE : (v + 1) * SIDE]
            result[v, x * SIDE : (x + 2) * SIDE] = jnp.concatenate(
                [rows[:, :LANES], rows[:, LANES:]], axis=0
            ).astype(BF16)
        part = pl.ds(x * SIDE, 2 * SIDE)
        write = pltpu.make_async_copy(
            result.at[:, part], out.at[:, part], out_sem.at[x // 2]
        )
        write.start()
        writes.append(write)

    for copy in sent + stiff_copies():
        copy.wait_send()

    @pl.loop(0, CHUNKS)
    def _(c):
        for app in range(2):
            for copy in face_copies(app, c):
                copy.wait_send()

    for write in writes:
        write.wait()


def on_device(sizes, nodes_total, panel_in, prior_modes, stiffness, mass_shift):
    nx, ny, nz = sizes
    tables = make_tables()
    low = (2, CHUNKS, 24 * PAIRS, 2 * LANES)
    high = (2, CHUNKS, 16 * PAIRS, 2 * LANES)
    flat = (2, CHUNKS, ROWS, LANES)
    any_space = pl.BlockSpec(memory_space=pl.ANY)
    dma = pltpu.SemaphoreType.DMA
    basis, upper = pl.pallas_call(
        functools.partial(kernel, sizes, nodes_total),
        out_shape=(
            jax.ShapeDtypeStruct((VECS, ROWS, LANES), BF16),
            jax.ShapeDtypeStruct((VECS, VECS), F32),
        ),
        in_specs=[any_space] * (4 + TABLES),
        out_specs=(any_space, pl.BlockSpec(memory_space=pltpu.VMEM)),
        scratch_shapes=[pltpu.VMEM(t.shape, t.dtype) for t in tables]
        + [
            pltpu.VMEM((VECS, ROWS, LANES), BF16),
            pltpu.VMEM((PRIOR, ROWS, LANES), BF16),
            pltpu.VMEM((ROWS, LANES), BF16),
            pltpu.VMEM((ROWS, LANES), BF16),
            pltpu.VMEM((VECS, ROWS, LANES), BF16),
            pltpu.VMEM(low, BF16),
            pltpu.VMEM(high, BF16),
            pltpu.VMEM(low, BF16),
            pltpu.VMEM(high, BF16),
            pltpu.VMEM(flat, BF16),
            pltpu.VMEM(low, BF16),
            pltpu.VMEM(high, BF16),
            pltpu.VMEM(low, BF16),
            pltpu.VMEM(high, BF16),
            pltpu.VMEM(flat, BF16),
            pltpu.VMEM(flat, BF16),
            pltpu.VMEM((6, ROWS, LANES), BF16),
            pltpu.VMEM((BLOCK, LANES), F32),
            pltpu.VMEM((ROWS, BLOCK), F32),
            pltpu.VMEM((ROWS, LANES), F32),
            pltpu.VMEM(((VECS + PRIOR) * SIDE, SIDE * LANES), BF16),
            pltpu.VMEM((PAIRS, BLOCK, 2 * LANES), BF16),
            pltpu.VMEM((CHUNK * ROWS, BLOCK), BF16),
            pltpu.VMEM((nz, 24, LANES), F32),
            pltpu.VMEM((nx, 24, LANES), F32),
            pltpu.VMEM((ny, 24, LANES), F32),
            pltpu.VMEM((VECS, ROWS, LANES), BF16),
            dma((3 + CHUNKS + TABLES,)),
            dma((SIDE // 2,)),
            dma((6,)),
            dma((6,)),
            dma((2, CHUNKS, 6)),
            dma((2, CHUNKS, 6)),
            dma((3, max(sizes))),
            dma((3, max(sizes))),
        ],
        compiler_params=pltpu.CompilerParams(
            collective_id=0, has_side_effects=True, vmem_limit_bytes=56 * 2**20
        ),
    )(
        panel_in.reshape(VECS, ROWS, LANES),
        prior_modes.reshape(PRIOR, ROWS, LANES),
        stiffness.reshape(ROWS, LANES),
        mass_shift.reshape(ROWS, LANES),
        *[jnp.asarray(t) for t in tables],
    )
    return basis.reshape(panel_in.shape), upper


def solution(mesh):
    sizes = tuple(mesh.shape[a] for a in ("gx", "gy", "gz"))
    nodes_total = ROWS * LANES * sizes[0] * sizes[1] * sizes[2]
    placed = (
        P(None, "gx", "gy", "gz"),
        P(None, "gx", "gy", "gz"),
        P("gx", "gy", "gz"),
        P("gx", "gy", "gz"),
    )
    return jax.shard_map(
        functools.partial(on_device, sizes, nodes_total),
        mesh=mesh,
        in_specs=placed,
        out_specs=(P(None, "gx", "gy", "gz"), P()),
        check_vma=False,
    )
```

```python
import functools

import jax
import jax.numpy as jnp
import ml_dtypes
import numpy as np
from jax import lax
from jax.experimental import pallas as pl
from jax.experimental.pallas import tpu as pltpu
from jax.sharding import PartitionSpec as P

filter_center = 10.0
filter_half = 12.0

MESH = pl.DeviceIdType.MESH
BF16 = jnp.bfloat16
F32 = jnp.float32
VECS = 32
PRIOR = 64
SIDE = 8
ROWS = SIDE * SIDE
LANES = 128
CHUNK = 8
CHUNKS = VECS // CHUNK
PAIRS = CHUNK // 2
SLOT = LANES // CHUNK
POINTS_Z = 5 * (LANES // 4 + 1)


def lobatto_tables():
    points = np.array([-1.0, -np.sqrt(3.0 / 7.0), 0.0, np.sqrt(3.0 / 7.0), 1.0])
    weights = np.array([0.1, 49.0 / 90.0, 32.0 / 45.0, 49.0 / 90.0, 0.1])
    scales = np.array(
        [np.prod([points[i] - points[k] for k in range(5) if k != i]) for i in range(5)]
    )
    derivative = np.zeros((5, 5))
    for i in range(5):
        for j in range(5):
            if j != i:
                derivative[i, j] = scales[i] / scales[j] / (points[i] - points[j])
        derivative[i, i] = -np.sum(derivative[i])
    return (derivative, weights)


def node_weight(count):
    weights = lobatto_tables()[1]
    per_node = [weights[3], weights[4] + weights[0], weights[1], weights[2]]
    return np.array([per_node[i % 4] for i in range(count)])


HIGH_X, HIGH_Y, LOW_X, LOW_Y = 64, 80, 96, 144
BLOCK = 256


def field_row(x, y, parity):
    if x < 0:
        return LOW_X + 24 * parity + (x + 3) * SIDE + y
    if y < 0:
        return LOW_Y + 24 * parity + (y + 3) * SIDE + x
    if x >= SIDE:
        return HIGH_X + (x - SIDE) * SIDE + y
    if y >= SIDE:
        return HIGH_Y + (y - SIDE) * SIDE + x
    return x * SIDE + y


def stiff_row(x, y):
    if x < 0:
        return ROWS + (x + SIDE) * SIDE + y
    if x >= SIDE:
        return 2 * ROWS + (x - SIDE) * SIDE + y
    if y < 0:
        return 3 * ROWS + x * SIDE + y + SIDE
    if y >= SIDE:
        return 4 * ROWS + x * SIDE + y - SIDE
    return x * SIDE + y


STIFF_K = 384


def make_tables():
    derivative, weights = lobatto_tables()
    node_w = node_weight(SIDE)
    node_z = node_weight(LANES)
    grad = np.zeros((2, BLOCK, BLOCK))
    back = np.zeros((ROWS, BLOCK))
    pick = np.zeros((BLOCK, STIFF_K))
    scale = np.zeros((BLOCK, LANES))
    for m in range(3):
        for q in range(5):
            for t in range(SIDE):
                rx = (m * 5 + q) * SIDE + t
                ry = 120 + rx
                at = 4 * m - 3 + q
                pick[rx, stiff_row(at, t)] = 1
                pick[ry, stiff_row(t, at)] = 1
                scale[rx] = weights[q] * node_w[t] * node_z
                scale[ry] = weights[q] * node_w[t] * node_z
                for a in range(5):
                    node = 4 * m - 3 + a
                    for parity in range(2):
                        grad[parity, rx, field_row(node, t, parity)] = derivative[q, a]
                        grad[parity, ry, field_row(t, node, parity)] = derivative[q, a]
                    if 0 <= node < SIDE:
                        back[node * SIDE + t, rx] = derivative[q, a]
                        back[t * SIDE + node, ry] = derivative[q, a]
    grad_z = np.zeros((2 * LANES, BLOCK))
    back_z = np.zeros((BLOCK, LANES))
    pick_z = np.zeros((3 * LANES, BLOCK))
    scale_z = np.zeros((ROWS, BLOCK))
    for m in range(LANES // 4 + 1):
        for q in range(5):
            col = 5 * m + q
            at = 4 * m - 3 + q
            source = at if 0 <= at < LANES else (2 * LANES + at if at < 0 else LANES + at)
            pick_z[source, col] = 1
            for t in range(ROWS):
                scale_z[t, col] = weights[q] * node_w[t // SIDE] * node_w[t % SIDE]
            for a in range(5):
                node = 4 * m - 3 + a
                row = node
                if node < 0:
                    row = LANES + node + 3
                elif node >= LANES:
                    row = LANES + 3 + node - LANES
                else:
                    back_z[col, node] = derivative[q, a]
                grad_z[row, col] = derivative[q, a]
    faces = np.zeros((128, 128))
    for half in range(2):
        for t in range(SIDE):
            for j in range(2):
                faces[16 * half + j * SIDE + t, 64 * half + t * SIDE + j] = 1
            for j in range(3):
                faces[32 + 24 * half + j * SIDE + t, 64 * half + (5 + j) * SIDE + t] = 1
                faces[80 + 24 * half + j * SIDE + t, 64 * half + t * SIDE + 5 + j] = 1
    volume = np.zeros((ROWS, LANES))
    for t in range(ROWS):
        volume[t] = node_w[t // SIDE] * node_w[t % SIDE] * node_z
    halves = [grad, back, pick, grad_z, back_z, pick_z, faces]
    singles = [scale, scale_z, volume]
    return [t.astype(np.float32).astype(ml_dtypes.bfloat16) for t in halves] + [
        t.astype(np.float32) for t in singles
    ]


def dot(a, b):
    return jnp.dot(a, b, preferred_element_type=F32)


def dot_nt(a, b, precision=None):
    return lax.dot_general(
        a, b, (((1,), (1,)), ((), ())), precision=precision, preferred_element_type=F32
    )


def side(shape, dim):
    return lax.broadcasted_iota(jnp.int32, shape, dim)


TABLES = 10


def kernel(sizes, nodes_total, *refs):
    panel, prior, stiff, mass = refs[:4]
    tables = refs[4 : 4 + TABLES]
    rows_out, sums_out = refs[4 + TABLES : 6 + TABLES]
    scratch = refs[6 + TABLES :]
    held = scratch[:TABLES]
    grad, back, pick, grad_z, back_z, pick_z, faces, scale, scale_z, volume = held
    (
        field,
        modes,
        stiff_own,
        mass_own,
        once,
        low_x_s,
        high_x_s,
        low_y_s,
        high_y_s,
        ends_s,
        low_x_r,
        high_x_r,
        low_y_r,
        high_y_r,
        low_z_r,
        high_z_r,
        stiff_r,
        factor,
        factor_z,
        shift,
        whole,
        image_rows,
        flux,
        flux_z,
        slots_z,
        slots_x,
        slots_y,
        load_sem,
        rows_sem,
        stiff_send,
        stiff_recv,
        face_send,
        face_recv,
        sum_send,
        sum_recv,
    ) = scratch[TABLES:]
    nx, ny, nz = sizes
    axes = ("gx", "gy", "gz")
    me = [lax.axis_index(a) for a in axes]

    def along(axis, step):
        return {axes[axis]: lax.rem(me[axis] + step + sizes[axis], sizes[axis])}

    barrier = pltpu.get_barrier_semaphore()
    for axis in range(3):
        for step in range(1, sizes[axis]):
            pl.semaphore_signal(
                barrier, inc=1, device_id=along(axis, step), device_id_type=MESH
            )
    loads = {}

    def load(name, src, dst):
        loads[name] = pltpu.make_async_copy(src, dst, load_sem.at[len(loads)])
        loads[name].start()

    def loaded(*names):
        for name in names:
            loads[name].wait()

    load("faces", tables[6], faces)
    load("stiff", stiff, stiff_own)
    for c in range(CHUNKS):
        part = pl.ds(c * CHUNK, CHUNK)
        load(c, panel.at[part], field.at[part])

    def pack(app, c, source):
        cells = [source[c * CHUNK + j] for j in range(CHUNK)]
        pairs = [
            jnp.concatenate([cells[2 * p], cells[2 * p + 1]], axis=1) for p in range(PAIRS)
        ]
        for p in range(PAIRS):
            high_x_s[app, c, 16 * p : 16 * p + 16] = pairs[p][:16]
        for q in range(PAIRS // 2):
            both = jnp.concatenate([pairs[2 * q], pairs[2 * q + 1]], axis=0)
            picked = dot(faces[...], both).astype(BF16)
            high_y_s[app, c, 32 * q : 32 * q + 32] = picked[:32]
            low_x_s[app, c, 48 * q : 48 * q + 48] = picked[32:80]
            low_y_s[app, c, 48 * q : 48 * q + 48] = picked[80:]
        lane = side((ROWS, LANES), 1)
        edges = jnp.zeros((ROWS, LANES), F32)
        for j in range(CHUNK):
            here = (lane >= SLOT * j) & (lane < SLOT * j + 5)
            edges = jnp.where(here, pltpu.roll(cells[j].astype(F32), SLOT * j + 3, 1), edges)
        ends_s[app, c] = edges.astype(BF16)

    def face_copies(app, c):
        plan = [
            (low_x_s, low_x_r, 0, 1),
            (high_x_s, high_x_r, 0, -1),
            (low_y_s, low_y_r, 1, 1),
            (high_y_s, high_y_r, 1, -1),
            (ends_s, low_z_r, 2, 1),
            (ends_s, high_z_r, 2, -1),
        ]
        return [
            pltpu.make_async_remote_copy(
                src_ref=src.at[app, c],
                dst_ref=dst.at[app, c],
                send_sem=face_send.at[app, c, k],
                recv_sem=face_recv.at[app, c, k],
                device_id=along(axis, step),
                device_id_type=MESH,
            )
            for k, (src, dst, axis, step) in enumerate(plan)
        ]

    def stiff_copies():
        return [
            pltpu.make_async_remote_copy(
                src_ref=stiff_own,
                dst_ref=stiff_r.at[k],
                send_sem=stiff_send.at[k],
                recv_sem=stiff_recv.at[k],
                device_id=along(k // 2, 1 - 2 * (k % 2)),
                device_id_type=MESH,
            )
            for k in range(6)
        ]

    loaded("faces", "stiff")
    for c in range(CHUNKS):
        loaded(c)
        if c == 0:
            for k in (0, 2, 3, 5, 7, 8, 9, 1, 4):
                load("table%d" % k, tables[k], held[k])
            load("mass", mass, mass_own)
            load("prior", prior, modes)
        pack(0, c, field)
        if c == 0:
            pl.semaphore_wait(barrier, nx + ny + nz - 3)
            for copy in stiff_copies():
                copy.start()
        for copy in face_copies(0, c):
            copy.start()

    loaded("table0", "table2", "table3", "table5")

    first = [me[k] == 0 for k in range(3)]
    last = [me[k] == sizes[k] - 1 for k in range(3)]

    def outside(index, spans):
        cut = index < 0
        for low, high, missing in spans:
            cut = cut | ((index >= low) & (index < high) & missing)
        return cut

    col = side((BLOCK, BLOCK), 1)
    cut = outside(
        col,
        [
            (HIGH_X, HIGH_Y, last[0]),
            (HIGH_Y, LOW_X, last[1]),
            (LOW_X, LOW_Y, first[0]),
            (LOW_Y, LOW_Y + 48, first[1]),
        ],
    )
    for parity in range(2):
        grad[parity] = jnp.where(cut, 0.0, grad[parity].astype(F32)).astype(BF16)
    row = side((2 * LANES, BLOCK), 0)
    cut = outside(row, [(LANES, LANES + 3, first[2]), (LANES + 3, LANES + 5, last[2])])
    grad_z[...] = jnp.where(cut, 0.0, grad_z[...].astype(F32)).astype(BF16)
    col = side((BLOCK, STIFF_K), 1)
    cut = outside(
        col,
        [
            (ROWS, 2 * ROWS, first[0]),
            (2 * ROWS, 3 * ROWS, last[0]),
            (3 * ROWS, 4 * ROWS, first[1]),
            (4 * ROWS, 5 * ROWS, last[1]),
        ],
    )
    pick[...] = jnp.where(cut, 0.0, pick[...].astype(F32)).astype(BF16)
    row = side((3 * LANES, BLOCK), 0)
    cut = outside(row, [(LANES, 2 * LANES, first[2]), (2 * LANES, 3 * LANES, last[2])])
    pick_z[...] = jnp.where(cut, 0.0, pick_z[...].astype(F32)).astype(BF16)

    loaded("table7", "table8", "table9", "mass")
    shift[...] = volume[...] * mass_own[...].astype(F32) + filter_center

    loaded("table1", "table4", "prior")

    def place(at, cells):
        for x in range(SIDE):
            rows = slice(x * SIDE, (x + 1) * SIDE)
            block = jnp.stack([cell[rows] for cell in cells], axis=0)
            block = jnp.swapaxes(block, 0, 1).astype(BF16)
            for y in range(SIDE):
                first_lane = (x * SIDE + y) * LANES
                whole[at, first_lane : first_lane + LANES] = block[y]

    @pl.loop(0, PRIOR // 16)
    def _(g):
        at = pl.ds(pl.multiple_of(VECS + 16 * g, 16), 16)
        place(at, [modes[16 * g + j].astype(F32) for j in range(16)])

    rows_writes = [
        pltpu.make_async_copy(whole.at[part], rows_out.at[part], rows_sem.at[k])
        for k, part in enumerate([pl.ds(VECS, PRIOR), pl.ds(0, VECS)])
    ]
    rows_writes[0].start()

    for copy in stiff_copies():
        copy.wait_recv()
    around = jnp.concatenate(
        [stiff_own[...]]
        + [stiff_r[k] for k in range(4)]
        + [jnp.zeros((STIFF_K - 5 * ROWS, LANES), BF16)],
        axis=0,
    )
    factor[...] = dot(pick[...], around) * scale[...]
    around = jnp.concatenate([stiff_own[...], stiff_r[4], stiff_r[5]], axis=1)
    factor_z[...] = dot(around, pick_z[...]) * scale_z[...]

    def operate(app, c, source, finish):
        slot = lax.rem(side((ROWS, LANES), 1), SLOT)
        joined = jnp.where(
            slot < 3, low_z_r[app, c].astype(F32), high_z_r[app, c].astype(F32)
        )
        cells = [source[c * CHUNK + j] for j in range(CHUNK)]
        lines = []
        for j in range(CHUNK):
            rolled = pltpu.roll(joined, LANES - SLOT * j, 1) if j else joined
            lines.append(jnp.concatenate([cells[j], rolled.astype(BF16)], axis=1))
        factor_rows = jnp.concatenate([factor_z[...]] * CHUNK, axis=0)
        flux_z[...] = (
            dot(jnp.concatenate(lines, axis=0), grad_z[...]) * factor_rows
        ).astype(BF16)
        factor_two = jnp.concatenate([factor[...], factor[...]], axis=1)
        for p in range(PAIRS):
            q, parity = p // 2, p % 2
            rows = jnp.concatenate(
                [
                    jnp.concatenate(cells[2 * p : 2 * p + 2], axis=1),
                    high_x_r[app, c, 16 * p : 16 * p + 16],
                    high_y_r[app, c, 16 * p : 16 * p + 16],
                    low_x_r[app, c, 48 * q : 48 * q + 48],
                    low_y_r[app, c, 48 * q : 48 * q + 48],
                    jnp.zeros((BLOCK - 192, 2 * LANES), BF16),
                ],
                axis=0,
            )
            flux[p] = (dot(grad[parity], rows) * factor_two).astype(BF16)
        image_z = dot(flux_z[...], back_z[...])
        for p in range(PAIRS):
            image = dot(back[...], flux[p])
            moved = [
                image[:, h * LANES : (h + 1) * LANES]
                + image_z[(2 * p + h) * ROWS : (2 * p + h + 1) * ROWS]
                - shift[...] * cells[2 * p + h].astype(F32)
                for h in range(2)
            ]
            finish(c, p, moved)

    def finish_one(c, p, moved):
        for h in range(2):
            once[c * CHUNK + 2 * p + h] = (moved[h] * (1.0 / filter_half)).astype(BF16)

    def finish_two(c, p, moved):
        for h in range(2):
            j = c * CHUNK + 2 * p + h
            done = moved[h] * (2.0 / filter_half) - field[j].astype(F32)
            image_rows[lax.rem(j, 16)] = done

    @pl.loop(0, CHUNKS)
    def _(c):
        for copy in face_copies(0, c):
            copy.wait_recv()
        operate(0, c, field, finish_one)
        pack(1, c, once)
        for copy in face_copies(1, c):
            copy.start()

    @pl.loop(0, VECS // 16)
    def _(g):
        for k in range(16 // CHUNK):
            c = g * (16 // CHUNK) + k
            for copy in face_copies(1, c):
                copy.wait_recv()
            operate(1, c, once, finish_two)
        at = pl.ds(pl.multiple_of(16 * g, 16), 16)
        place(at, [image_rows[j] for j in range(16)])

    rows_writes[1].start()
    sums = dot_nt(whole[:VECS], whole[...])
    sums = jnp.concatenate([sums, jnp.zeros((VECS, LANES - VECS - PRIOR), F32)], axis=1)

    lane = side((8, LANES), 1)
    used = VECS + PRIOR
    tail = sums[24:]
    mine = jnp.concatenate(
        [
            jnp.where(lane < used, sums[8 * r : 8 * r + 8], pltpu.roll(tail, used - 32 * r, 1))
            for r in range(3)
        ],
        axis=0,
    )
    sent = []
    for stage, (axis, slots) in enumerate(((2, slots_z), (0, slots_x), (1, slots_y))):
        slots[me[axis]] = mine
        here = slots.at[me[axis]]
        copies = [
            pltpu.make_async_remote_copy(
                src_ref=here,
                dst_ref=here,
                send_sem=sum_send.at[stage, step],
                recv_sem=sum_recv.at[stage, step],
                device_id=along(axis, step),
                device_id_type=MESH,
            )
            for step in range(1, sizes[axis])
        ]
        for copy in copies:
            copy.start()
        for copy in copies:
            copy.wait_recv()
        sent += copies
        mine = slots[0]
        for k in range(1, sizes[axis]):
            mine = mine + slots[k]
    tail = jnp.zeros((8, LANES), F32)
    for r in range(3):
        part = pltpu.roll(mine[8 * r : 8 * r + 8], LANES - used + 32 * r, 1)
        tail = jnp.where((lane >= 32 * r) & (lane < 32 * r + 32), part, tail)
    sums_out[...] = jnp.concatenate([mine, tail], axis=0)

    for copy in sent + stiff_copies():
        copy.wait_send()

    @pl.loop(0, CHUNKS)
    def _(c):
        for app in range(2):
            for copy in face_copies(app, c):
                copy.wait_send()

    for write in rows_writes:
        write.wait()


def finish_kernel(nodes_total, rows_in, sums_in, out, upper, whole, result, rows_sem, out_sem):
    width = 2 * SIDE * LANES
    parts = SIDE // 2
    loads = []
    for k in range(parts):
        part = pl.ds(k * width, width)
        load = pltpu.make_async_copy(rows_in.at[:, part], whole.at[:, part], rows_sem.at[k])
        load.start()
        loads.append(load)

    lane = side((VECS, LANES), 1)
    line = side((VECS, LANES), 0)
    sums = sums_in[...] * (1.0 / nodes_total)
    proj = jnp.where((lane >= VECS) & (lane < VECS + PRIOR), sums, 0.0)
    coeffs = proj.astype(BF16)
    rest = proj - coeffs.astype(F32)
    rest_high = rest.astype(BF16)
    rest_low = (rest - rest_high.astype(F32)).astype(BF16)
    left = jnp.concatenate([coeffs, coeffs, coeffs, rest_high, rest_low], axis=1)
    right = jnp.concatenate([coeffs, rest_high, rest_low, coeffs, coeffs], axis=1)
    right = jnp.concatenate([right, jnp.zeros((LANES - VECS, 5 * LANES), BF16)], axis=0)
    state = jnp.where(lane < VECS, sums - dot_nt(left, right), 0.0)
    state = jnp.where(lane == line + VECS, 1.0, state)
    state = state - pltpu.roll(coeffs.astype(F32), VECS, 1)

    step = 8

    def rows_of(value):
        return jnp.concatenate([value] * (VECS // 8), axis=0)

    for first in range(0, VECS, step):
        cols = [
            jnp.broadcast_to(state[:, first + j : first + j + 1], (VECS, LANES))
            for j in range(step)
        ]
        lines = [
            jnp.broadcast_to(state[first + j : first + j + 1], (8, LANES)) for j in range(step)
        ]
        pivots = [
            [jnp.broadcast_to(cols[j][first + i : first + i + 1], (8, LANES)) for j in range(step)]
            for i in range(step)
        ]
        ratios = []
        for j in range(step):
            inverse = 1.0 / pivots[j][j]
            ratio = jnp.where(line > first + j, cols[j] * rows_of(inverse), 0.0)
            ratios.append(ratio)
            for i in range(j + 1, step):
                times = pivots[i][j] * inverse
                for t in range(j + 1, step):
                    pivots[i][t] = pivots[i][t] - times * pivots[j][t]
                lines[i] = lines[i] - times * lines[j]
                cols[i] = cols[i] - ratio * rows_of(pivots[j][i])
        for j in range(step):
            state = state - ratios[j] * rows_of(lines[j])
    diagonal = jnp.sum(jnp.where(lane == line, state, 0.0), axis=1, keepdims=True)
    state = state * (1.0 / jnp.sqrt(diagonal))
    upper[...] = jnp.where(lane >= line, state, 0.0)[:, :VECS]

    solve = pltpu.roll(state, LANES - VECS, 1)[:, : VECS + PRIOR]
    high = solve.astype(BF16)
    low = (solve - high.astype(F32)).astype(BF16)
    solve = jnp.concatenate([high, low], axis=0)
    writes = []
    for k in range(parts):
        loads[k].wait()
        blocks = []
        for x in (2 * k, 2 * k + 1):
            block = dot(solve, whole[:, x * SIDE * LANES : (x + 1) * SIDE * LANES])
            block = block[:VECS] + block[VECS:]
            block = jnp.stack(
                [block[:, y * LANES : (y + 1) * LANES] for y in range(SIDE)], axis=0
            )
            blocks.append(jnp.swapaxes(block, 0, 1))
        at = slice(2 * k * SIDE, 2 * (k + 1) * SIDE)
        for v in range(VECS):
            result[v, at] = jnp.concatenate([blocks[0][v], blocks[1][v]], axis=0).astype(BF16)
        part = pl.ds(2 * k * SIDE, 2 * SIDE)
        write = pltpu.make_async_copy(result.at[:, part], out.at[:, part], out_sem.at[k])
        write.start()
        writes.append(write)
    for write in writes:
        write.wait()


def on_device(sizes, nodes_total, panel_in, prior_modes, stiffness, mass_shift):
    nx, ny, nz = sizes
    tables = make_tables()
    low = (2, CHUNKS, 24 * PAIRS, 2 * LANES)
    high = (2, CHUNKS, 16 * PAIRS, 2 * LANES)
    flat = (2, CHUNKS, ROWS, LANES)
    any_space = pl.BlockSpec(memory_space=pl.ANY)
    dma = pltpu.SemaphoreType.DMA
    rows, sums = pl.pallas_call(
        functools.partial(kernel, sizes, nodes_total),
        out_shape=(
            jax.ShapeDtypeStruct((VECS + PRIOR, ROWS * LANES), BF16),
            jax.ShapeDtypeStruct((VECS, LANES), F32),
        ),
        in_specs=[any_space] * (4 + TABLES),
        out_specs=(any_space, pl.BlockSpec(memory_space=pltpu.VMEM)),
        scratch_shapes=[pltpu.VMEM(t.shape, t.dtype) for t in tables]
        + [
            pltpu.VMEM((VECS, ROWS, LANES), BF16),
            pltpu.VMEM((PRIOR, ROWS, LANES), BF16),
            pltpu.VMEM((ROWS, LANES), BF16),
            pltpu.VMEM((ROWS, LANES), BF16),
            pltpu.VMEM((VECS, ROWS, LANES), BF16),
            pltpu.VMEM(low, BF16),
            pltpu.VMEM(high, BF16),
            pltpu.VMEM(low, BF16),
            pltpu.VMEM(high, BF16),
            pltpu.VMEM(flat, BF16),
            pltpu.VMEM(low, BF16),
            pltpu.VMEM(high, BF16),
            pltpu.VMEM(low, BF16),
            pltpu.VMEM(high, BF16),
            pltpu.VMEM(flat, BF16),
            pltpu.VMEM(flat, BF16),
            pltpu.VMEM((6, ROWS, LANES), BF16),
            pltpu.VMEM((BLOCK, LANES), F32),
            pltpu.VMEM((ROWS, BLOCK), F32),
            pltpu.VMEM((ROWS, LANES), F32),
            pltpu.VMEM((VECS + PRIOR, ROWS * LANES), BF16),
            pltpu.VMEM((16, ROWS, LANES), F32),
            pltpu.VMEM((PAIRS, BLOCK, 2 * LANES), BF16),
            pltpu.VMEM((CHUNK * ROWS, BLOCK), BF16),
            pltpu.VMEM((nz, 24, LANES), F32),
            pltpu.VMEM((nx, 24, LANES), F32),
            pltpu.VMEM((ny, 24, LANES), F32),
            dma((3 + CHUNKS + TABLES,)),
            dma((2,)),
            dma((6,)),
            dma((6,)),
            dma((2, CHUNKS, 6)),
            dma((2, CHUNKS, 6)),
            dma((3, max(sizes))),
            dma((3, max(sizes))),
        ],
        compiler_params=pltpu.CompilerParams(
            collective_id=0, has_side_effects=True, vmem_limit_bytes=56 * 2**20
        ),
    )(
        panel_in.reshape(VECS, ROWS, LANES),
        prior_modes.reshape(PRIOR, ROWS, LANES),
        stiffness.reshape(ROWS, LANES),
        mass_shift.reshape(ROWS, LANES),
        *[jnp.asarray(t) for t in tables],
    )
    basis, upper = pl.pallas_call(
        functools.partial(finish_kernel, nodes_total),
        out_shape=(
            jax.ShapeDtypeStruct((VECS, ROWS, LANES), BF16),
            jax.ShapeDtypeStruct((VECS, VECS), F32),
        ),
        in_specs=[any_space, pl.BlockSpec(memory_space=pltpu.VMEM)],
        out_specs=(any_space, pl.BlockSpec(memory_space=pltpu.VMEM)),
        scratch_shapes=[
            pltpu.VMEM((VECS + PRIOR, ROWS * LANES), BF16),
            pltpu.VMEM((VECS, ROWS, LANES), BF16),
            dma((SIDE // 2,)),
            dma((SIDE // 2,)),
        ],
        compiler_params=pltpu.CompilerParams(vmem_limit_bytes=56 * 2**20),
    )(rows, sums)
    return basis.reshape(panel_in.shape), upper


def solution(mesh):
    sizes = tuple(mesh.shape[a] for a in ("gx", "gy", "gz"))
    nodes_total = ROWS * LANES * sizes[0] * sizes[1] * sizes[2]
    placed = (
        P(None, "gx", "gy", "gz"),
        P(None, "gx", "gy", "gz"),
        P("gx", "gy", "gz"),
        P("gx", "gy", "gz"),
    )
    return jax.shard_map(
        functools.partial(on_device, sizes, nodes_total),
        mesh=mesh,
        in_specs=placed,
        out_specs=(P(None, "gx", "gy", "gz"), P()),
        check_vma=False,
    )
```

```python
import functools

import jax
import jax.numpy as jnp
import ml_dtypes
import numpy as np
from jax import lax
from jax.experimental import pallas as pl
from jax.experimental.pallas import tpu as pltpu
from jax.sharding import PartitionSpec as P

filter_center = 10.0
filter_half = 12.0

MESH = pl.DeviceIdType.MESH
BF16 = jnp.bfloat16
F32 = jnp.float32
VECS = 32
PRIOR = 64
SIDE = 8
ROWS = SIDE * SIDE
LANES = 128
CHUNK = 8
CHUNKS = VECS // CHUNK
PAIRS = CHUNK // 2
SLOT = LANES // CHUNK
POINTS_Z = 5 * (LANES // 4 + 1)


def lobatto_tables():
    points = np.array([-1.0, -np.sqrt(3.0 / 7.0), 0.0, np.sqrt(3.0 / 7.0), 1.0])
    weights = np.array([0.1, 49.0 / 90.0, 32.0 / 45.0, 49.0 / 90.0, 0.1])
    scales = np.array(
        [np.prod([points[i] - points[k] for k in range(5) if k != i]) for i in range(5)]
    )
    derivative = np.zeros((5, 5))
    for i in range(5):
        for j in range(5):
            if j != i:
                derivative[i, j] = scales[i] / scales[j] / (points[i] - points[j])
        derivative[i, i] = -np.sum(derivative[i])
    return (derivative, weights)


def node_weight(count):
    weights = lobatto_tables()[1]
    per_node = [weights[3], weights[4] + weights[0], weights[1], weights[2]]
    return np.array([per_node[i % 4] for i in range(count)])


HIGH_X, HIGH_Y, LOW_X, LOW_Y = 64, 80, 96, 144
BLOCK = 256
LOW_X_R, LOW_Y_R, HIGH_X_R, HIGH_Y_R = 0, 96, 192, 256


def field_row(x, y, parity):
    if x < 0:
        return LOW_X + 24 * parity + (x + 3) * SIDE + y
    if y < 0:
        return LOW_Y + 24 * parity + (y + 3) * SIDE + x
    if x >= SIDE:
        return HIGH_X + (x - SIDE) * SIDE + y
    if y >= SIDE:
        return HIGH_Y + (y - SIDE) * SIDE + x
    return x * SIDE + y


def stiff_row(x, y):
    if x < 0:
        return ROWS + (x + SIDE) * SIDE + y
    if x >= SIDE:
        return 2 * ROWS + (x - SIDE) * SIDE + y
    if y < 0:
        return 3 * ROWS + x * SIDE + y + SIDE
    if y >= SIDE:
        return 4 * ROWS + x * SIDE + y - SIDE
    return x * SIDE + y


STIFF_K = 384


def make_tables():
    derivative, weights = lobatto_tables()
    node_w = node_weight(SIDE)
    node_z = node_weight(LANES)
    grad = np.zeros((2, BLOCK, BLOCK))
    back = np.zeros((ROWS, BLOCK))
    pick = np.zeros((BLOCK, STIFF_K))
    scale = np.zeros((BLOCK, LANES))
    for m in range(3):
        for q in range(5):
            for t in range(SIDE):
                rx = (m * 5 + q) * SIDE + t
                ry = 120 + rx
                at = 4 * m - 3 + q
                pick[rx, stiff_row(at, t)] = 1
                pick[ry, stiff_row(t, at)] = 1
                scale[rx] = weights[q] * node_w[t] * node_z
                scale[ry] = weights[q] * node_w[t] * node_z
                for a in range(5):
                    node = 4 * m - 3 + a
                    for parity in range(2):
                        grad[parity, rx, field_row(node, t, parity)] = derivative[q, a]
                        grad[parity, ry, field_row(t, node, parity)] = derivative[q, a]
                    if 0 <= node < SIDE:
                        back[node * SIDE + t, rx] = derivative[q, a]
                        back[t * SIDE + node, ry] = derivative[q, a]
    grad_z = np.zeros((2 * LANES, BLOCK))
    back_z = np.zeros((BLOCK, LANES))
    pick_z = np.zeros((3 * LANES, BLOCK))
    scale_z = np.zeros((ROWS, BLOCK))
    for m in range(LANES // 4 + 1):
        for q in range(5):
            col = 5 * m + q
            at = 4 * m - 3 + q
            source = at if 0 <= at < LANES else (2 * LANES + at if at < 0 else LANES + at)
            pick_z[source, col] = 1
            for t in range(ROWS):
                scale_z[t, col] = weights[q] * node_w[t // SIDE] * node_w[t % SIDE]
            for a in range(5):
                node = 4 * m - 3 + a
                row = node
                if node < 0:
                    row = LANES + node + 3
                elif node >= LANES:
                    row = LANES + 3 + node - LANES
                else:
                    back_z[col, node] = derivative[q, a]
                grad_z[row, col] = derivative[q, a]
    faces = np.zeros((128, 128))
    for half in range(2):
        for t in range(SIDE):
            for j in range(2):
                faces[16 * half + j * SIDE + t, 64 * half + t * SIDE + j] = 1
            for j in range(3):
                faces[32 + 24 * half + j * SIDE + t, 64 * half + (5 + j) * SIDE + t] = 1
                faces[80 + 24 * half + j * SIDE + t, 64 * half + t * SIDE + 5 + j] = 1
    volume = np.zeros((ROWS, LANES))
    for t in range(ROWS):
        volume[t] = node_w[t // SIDE] * node_w[t % SIDE] * node_z
    halves = [grad, back, pick, grad_z, back_z, pick_z, faces]
    singles = [scale, scale_z, volume]
    return [t.astype(np.float32).astype(ml_dtypes.bfloat16) for t in halves] + [
        t.astype(np.float32) for t in singles
    ]


def dot(a, b):
    return jnp.dot(a, b, preferred_element_type=F32)


def dot_nt(a, b, precision=None):
    return lax.dot_general(
        a, b, (((1,), (1,)), ((), ())), precision=precision, preferred_element_type=F32
    )


def side(shape, dim):
    return lax.broadcasted_iota(jnp.int32, shape, dim)


TABLES = 10


def kernel(sizes, nodes_total, *refs):
    panel, prior, stiff, mass = refs[:4]
    tables = refs[4 : 4 + TABLES]
    whole, sums_out = refs[4 + TABLES : 6 + TABLES]
    scratch = refs[6 + TABLES :]
    held = scratch[:TABLES]
    grad, back, pick, grad_z, back_z, pick_z, faces, scale, scale_z, volume = held
    (
        field,
        modes,
        stiff_own,
        mass_own,
        once,
        low_x_s,
        low_y_s,
        high_x_s,
        high_y_s,
        ends_s,
        faces_r,
        ends_r,
        stiff_r,
        factor,
        factor_z,
        shift,
        image_rows,
        flux,
        flux_z,
        slots_z,
        slots_x,
        slots_y,
        load_sem,
        send_sem,
        recv_sem,
        stiff_sem,
        sum_send,
        sum_recv,
        token,
    ) = scratch[TABLES:]
    nx, ny, nz = sizes
    axes = ("gx", "gy", "gz")
    me = [lax.axis_index(a) for a in axes]

    def along(axis, step):
        return {axes[axis]: lax.rem(me[axis] + step + sizes[axis], sizes[axis])}

    barrier = pltpu.get_barrier_semaphore()

    def greet(semaphore):
        for axis in range(3):
            for step in (1, -1):
                pl.semaphore_signal(
                    semaphore, inc=1, device_id=along(axis, step), device_id_type=MESH
                )

    greet(barrier)
    loads = {}

    def load(name, src, dst):
        loads[name] = pltpu.make_async_copy(src, dst, load_sem.at[len(loads)])
        loads[name].start()

    def loaded(*names):
        for name in names:
            loads[name].wait()

    load("faces", tables[6], faces)
    load("stiff", stiff, stiff_own)
    for c in range(CHUNKS):
        part = pl.ds(c * CHUNK, CHUNK)
        load(c, panel.at[part], field.at[part])

    def pack(app, c, source):
        cells = [source[c * CHUNK + j] for j in range(CHUNK)]
        pairs = [
            jnp.concatenate([cells[2 * p], cells[2 * p + 1]], axis=1) for p in range(PAIRS)
        ]
        for p in range(PAIRS):
            high_x_s[app, c, 16 * p : 16 * p + 16] = pairs[p][:16]
        for q in range(PAIRS // 2):
            both = jnp.concatenate([pairs[2 * q], pairs[2 * q + 1]], axis=0)
            picked = dot(faces[...], both).astype(BF16)
            high_y_s[app, c, 32 * q : 32 * q + 32] = picked[:32]
            low_x_s[app, c, 48 * q : 48 * q + 48] = picked[32:80]
            low_y_s[app, c, 48 * q : 48 * q + 48] = picked[80:]
        lane = side((ROWS, LANES), 1)
        edges = jnp.zeros((ROWS, LANES), F32)
        for j in range(CHUNK):
            here = (lane >= SLOT * j) & (lane < SLOT * j + 5)
            edges = jnp.where(here, pltpu.roll(cells[j].astype(F32), SLOT * j + 3, 1), edges)
        ends_s[app, c] = edges.astype(BF16)

    def face_copies(app, c):
        plan = [
            (low_x_s, LOW_X_R, 0, 1),
            (high_x_s, HIGH_X_R, 0, -1),
            (low_y_s, LOW_Y_R, 1, 1),
            (high_y_s, HIGH_Y_R, 1, -1),
            (ends_s, 0, 2, 1),
            (ends_s, 1, 2, -1),
        ]
        copies = []
        for k, (src, at, axis, step) in enumerate(plan):
            if axis == 2:
                target = ends_r.at[app, c, at]
            else:
                target = faces_r.at[app, c, pl.ds(at, src.shape[2])]
            copies.append(
                pltpu.make_async_remote_copy(
                    src_ref=src.at[app, c],
                    dst_ref=target,
                    send_sem=send_sem.at[k],
                    recv_sem=recv_sem.at[app, c, axis // 2],
                    device_id=along(axis, step),
                    device_id_type=MESH,
                )
            )
        return copies

    def arrived(buffer, semaphore):
        pltpu.make_async_copy(buffer, buffer, semaphore).wait()

    def faces_arrived(app, c):
        arrived(faces_r.at[app, c], recv_sem.at[app, c, 0])
        arrived(ends_r.at[app, c], recv_sem.at[app, c, 1])

    def stiff_copies():
        return [
            pltpu.make_async_remote_copy(
                src_ref=stiff_own,
                dst_ref=stiff_r.at[k],
                send_sem=stiff_sem.at[0],
                recv_sem=stiff_sem.at[1],
                device_id=along(k // 2, 1 - 2 * (k % 2)),
                device_id_type=MESH,
            )
            for k in range(6)
        ]

    loaded("faces", "stiff")
    for c in range(CHUNKS):
        loaded(c)
        if c == 0:
            for k in (0, 2, 3, 5, 7, 8, 9, 1, 4):
                load("table%d" % k, tables[k], held[k])
            load("mass", mass, mass_own)
            load("prior", prior, modes)
        pack(0, c, field)
        if c == 0:
            pl.semaphore_wait(barrier, 6)
            for copy in stiff_copies():
                copy.start()
        for copy in face_copies(0, c):
            copy.start()

    loaded("table0", "table2", "table3", "table5")

    first = [me[k] == 0 for k in range(3)]
    last = [me[k] == sizes[k] - 1 for k in range(3)]

    def outside(index, spans):
        cut = index < 0
        for low, high, missing in spans:
            cut = cut | ((index >= low) & (index < high) & missing)
        return cut

    col = side((BLOCK, BLOCK), 1)
    cut = outside(
        col,
        [
            (HIGH_X, HIGH_Y, last[0]),
            (HIGH_Y, LOW_X, last[1]),
            (LOW_X, LOW_Y, first[0]),
            (LOW_Y, LOW_Y + 48, first[1]),
        ],
    )
    for parity in range(2):
        grad[parity] = jnp.where(cut, 0.0, grad[parity].astype(F32)).astype(BF16)
    row = side((2 * LANES, BLOCK), 0)
    cut = outside(row, [(LANES, LANES + 3, first[2]), (LANES + 3, LANES + 5, last[2])])
    grad_z[...] = jnp.where(cut, 0.0, grad_z[...].astype(F32)).astype(BF16)
    col = side((BLOCK, STIFF_K), 1)
    cut = outside(
        col,
        [
            (ROWS, 2 * ROWS, first[0]),
            (2 * ROWS, 3 * ROWS, last[0]),
            (3 * ROWS, 4 * ROWS, first[1]),
            (4 * ROWS, 5 * ROWS, last[1]),
        ],
    )
    pick[...] = jnp.where(cut, 0.0, pick[...].astype(F32)).astype(BF16)
    row = side((3 * LANES, BLOCK), 0)
    cut = outside(row, [(LANES, 2 * LANES, first[2]), (2 * LANES, 3 * LANES, last[2])])
    pick_z[...] = jnp.where(cut, 0.0, pick_z[...].astype(F32)).astype(BF16)

    loaded("table7", "table8", "table9", "mass")
    shift[...] = volume[...] * mass_own[...].astype(F32) + filter_center

    loaded("table1", "table4", "prior")

    def place(at, cells):
        for x in range(SIDE):
            rows = slice(x * SIDE, (x + 1) * SIDE)
            block = jnp.stack([cell[rows] for cell in cells], axis=0)
            block = jnp.swapaxes(block, 0, 1).astype(BF16)
            for y in range(SIDE):
                first_lane = (x * SIDE + y) * LANES
                whole[at, first_lane : first_lane + LANES] = block[y]

    @pl.loop(0, PRIOR // 16)
    def _(g):
        at = pl.ds(pl.multiple_of(VECS + 16 * g, 16), 16)
        place(at, [modes[16 * g + j].astype(F32) for j in range(16)])

    arrived(stiff_r, stiff_sem.at[1])
    around = jnp.concatenate(
        [stiff_own[...]]
        + [stiff_r[k] for k in range(4)]
        + [jnp.zeros((STIFF_K - 5 * ROWS, LANES), BF16)],
        axis=0,
    )
    factor[...] = dot(pick[...], around) * scale[...]
    around = jnp.concatenate([stiff_own[...], stiff_r[4], stiff_r[5]], axis=1)
    factor_z[...] = dot(around, pick_z[...]) * scale_z[...]

    def operate(app, c, source, finish):
        slot = lax.rem(side((ROWS, LANES), 1), SLOT)
        joined = jnp.where(
            slot < 3, ends_r[app, c, 0].astype(F32), ends_r[app, c, 1].astype(F32)
        )
        cells = [source[c * CHUNK + j] for j in range(CHUNK)]
        lines = []
        for j in range(CHUNK):
            rolled = pltpu.roll(joined, LANES - SLOT * j, 1) if j else joined
            lines.append(jnp.concatenate([cells[j], rolled.astype(BF16)], axis=1))
        factor_rows = jnp.concatenate([factor_z[...]] * CHUNK, axis=0)
        flux_z[...] = (
            dot(jnp.concatenate(lines, axis=0), grad_z[...]) * factor_rows
        ).astype(BF16)
        factor_two = jnp.concatenate([factor[...], factor[...]], axis=1)
        for p in range(PAIRS):
            q, parity = p // 2, p % 2
            rows = jnp.concatenate(
                [
                    jnp.concatenate(cells[2 * p : 2 * p + 2], axis=1),
                    faces_r[app, c, HIGH_X_R + 16 * p : HIGH_X_R + 16 * p + 16],
                    faces_r[app, c, HIGH_Y_R + 16 * p : HIGH_Y_R + 16 * p + 16],
                    faces_r[app, c, LOW_X_R + 48 * q : LOW_X_R + 48 * q + 48],
                    faces_r[app, c, LOW_Y_R + 48 * q : LOW_Y_R + 48 * q + 48],
                    jnp.zeros((BLOCK - 192, 2 * LANES), BF16),
                ],
                axis=0,
            )
            flux[p] = (dot(grad[parity], rows) * factor_two).astype(BF16)
        image_z = dot(flux_z[...], back_z[...])
        for p in range(PAIRS):
            image = dot(back[...], flux[p])
            moved = [
                image[:, h * LANES : (h + 1) * LANES]
                + image_z[(2 * p + h) * ROWS : (2 * p + h + 1) * ROWS]
                - shift[...] * cells[2 * p + h].astype(F32)
                for h in range(2)
            ]
            finish(c, p, moved)

    def finish_one(c, p, moved):
        for h in range(2):
            once[c * CHUNK + 2 * p + h] = (moved[h] * (1.0 / filter_half)).astype(BF16)

    def finish_two(c, p, moved):
        for h in range(2):
            j = c * CHUNK + 2 * p + h
            done = moved[h] * (2.0 / filter_half) - field[j].astype(F32)
            image_rows[lax.rem(j, 16)] = done

    @pl.loop(0, CHUNKS)
    def _(c):
        faces_arrived(0, c)
        operate(0, c, field, finish_one)
        pack(1, c, once)
        for copy in face_copies(1, c):
            copy.start()

    @pl.loop(0, VECS // 16)
    def _(g):
        for k in range(16 // CHUNK):
            c = g * (16 // CHUNK) + k
            faces_arrived(1, c)
            if k == 0:
                @pl.when(g == 0)
                def _():
                    greet(token.at[0])

            operate(1, c, once, finish_two)
        at = pl.ds(pl.multiple_of(16 * g, 16), 16)
        place(at, [image_rows[j] for j in range(16)])

    sums = dot_nt(whole[:VECS], whole[...])
    sums = jnp.concatenate([sums, jnp.zeros((VECS, LANES - VECS - PRIOR), F32)], axis=1)

    lane = side((8, LANES), 1)
    used = VECS + PRIOR
    tail = sums[24:]
    mine = jnp.concatenate(
        [
            jnp.where(lane < used, sums[8 * r : 8 * r + 8], pltpu.roll(tail, used - 32 * r, 1))
            for r in range(3)
        ],
        axis=0,
    )
    pl.semaphore_wait(token.at[0], 6)
    for stage, (axis, slots) in enumerate(((2, slots_z), (0, slots_x), (1, slots_y))):
        size = sizes[axis]
        slots[0] = mine
        steps = sorted(range(1, size), key=lambda step: -min(step, size - step))
        for step in steps:
            pltpu.make_async_remote_copy(
                src_ref=slots.at[0],
                dst_ref=slots.at[step],
                send_sem=sum_send.at[stage],
                recv_sem=sum_recv.at[stage],
                device_id=along(axis, step),
                device_id_type=MESH,
            ).start()
        arrived(slots.at[pl.ds(1, size - 1)], sum_recv.at[stage])
        parts = [slots[lax.rem(me[axis] - k + size, size)] for k in range(size)]
        mine = parts[0]
        for part in parts[1:]:
            mine = mine + part
    tail = jnp.zeros((8, LANES), F32)
    for r in range(3):
        part = pltpu.roll(mine[8 * r : 8 * r + 8], LANES - used + 32 * r, 1)
        tail = jnp.where((lane >= 32 * r) & (lane < 32 * r + 32), part, tail)
    sums_out[...] = jnp.concatenate([mine, tail], axis=0)

    for k, buffer in enumerate([low_x_s, high_x_s, low_y_s, high_y_s, ends_s, ends_s]):
        arrived(buffer, send_sem.at[k])
    arrived(stiff_r, stiff_sem.at[0])
    for stage, slots in enumerate((slots_z, slots_x, slots_y)):
        arrived(slots.at[pl.ds(1, slots.shape[0] - 1)], sum_send.at[stage])


def finish_kernel(nodes_total, whole, sums_in, out, upper_out, result, upper, out_sem):
    lane = side((VECS, LANES), 1)
    line = side((VECS, LANES), 0)
    sums = sums_in[...] * (1.0 / nodes_total)
    proj = jnp.where((lane >= VECS) & (lane < VECS + PRIOR), sums, 0.0)
    coeffs = proj.astype(BF16)
    rest = proj - coeffs.astype(F32)
    rest_high = rest.astype(BF16)
    rest_low = (rest - rest_high.astype(F32)).astype(BF16)
    left = jnp.concatenate([coeffs, coeffs, coeffs, rest_high, rest_low], axis=1)
    right = jnp.concatenate([coeffs, rest_high, rest_low, coeffs, coeffs], axis=1)
    right = jnp.concatenate([right, jnp.zeros((LANES - VECS, 5 * LANES), BF16)], axis=0)
    state = jnp.where(lane < VECS, sums - dot_nt(left, right), 0.0)
    state = jnp.where(lane == line + VECS, 1.0, state)
    state = state - pltpu.roll(coeffs.astype(F32), VECS, 1)

    step = 8

    def rows_of(value):
        return jnp.concatenate([value] * (VECS // 8), axis=0)

    for first in range(0, VECS, step):
        cols = [
            jnp.broadcast_to(state[:, first + j : first + j + 1], (VECS, LANES))
            for j in range(step)
        ]
        lines = [
            jnp.broadcast_to(state[first + j : first + j + 1], (8, LANES)) for j in range(step)
        ]
        pivots = [
            [jnp.broadcast_to(cols[j][first + i : first + i + 1], (8, LANES)) for j in range(step)]
            for i in range(step)
        ]
        ratios = []
        for j in range(step):
            inverse = 1.0 / pivots[j][j]
            ratio = jnp.where(line > first + j, cols[j] * rows_of(inverse), 0.0)
            ratios.append(ratio)
            for i in range(j + 1, step):
                times = pivots[i][j] * inverse
                for t in range(j + 1, step):
                    pivots[i][t] = pivots[i][t] - times * pivots[j][t]
                lines[i] = lines[i] - times * lines[j]
                cols[i] = cols[i] - ratio * rows_of(pivots[j][i])
        for j in range(step):
            state = state - ratios[j] * rows_of(lines[j])
    diagonal = jnp.sum(jnp.where(lane == line, state, 0.0), axis=1, keepdims=True)
    state = state * (1.0 / jnp.sqrt(diagonal))
    upper[...] = jnp.where(lane >= line, state, 0.0)[:, :VECS]
    writes = [pltpu.make_async_copy(upper, upper_out, out_sem.at[0])]
    writes[0].start()

    solve = pltpu.roll(state, LANES - VECS, 1)[:, : VECS + PRIOR]
    high = solve.astype(BF16)
    low = (solve - high.astype(F32)).astype(BF16)
    solve = jnp.concatenate([high, low], axis=0)
    for k in range(SIDE // 2):
        blocks = []
        for x in (2 * k, 2 * k + 1):
            block = dot(solve, whole[:, x * SIDE * LANES : (x + 1) * SIDE * LANES])
            block = block[:VECS] + block[VECS:]
            block = jnp.stack(
                [block[:, y * LANES : (y + 1) * LANES] for y in range(SIDE)], axis=0
            )
            blocks.append(jnp.swapaxes(block, 0, 1))
        at = slice(2 * k * SIDE, 2 * (k + 1) * SIDE)
        for v in range(VECS):
            result[v, at] = jnp.concatenate([blocks[0][v], blocks[1][v]], axis=0).astype(BF16)
        part = pl.ds(2 * k * SIDE, 2 * SIDE)
        write = pltpu.make_async_copy(result.at[:, part], out.at[:, part], out_sem.at[1 + k])
        write.start()
        writes.append(write)
    for write in writes:
        write.wait()


def on_device(sizes, nodes_total, panel_in, prior_modes, stiffness, mass_shift):
    nx, ny, nz = sizes
    tables = make_tables()
    low = (2, CHUNKS, 24 * PAIRS, 2 * LANES)
    high = (2, CHUNKS, 16 * PAIRS, 2 * LANES)
    hbm = pl.BlockSpec(memory_space=pltpu.HBM)
    vmem = pl.BlockSpec(memory_space=pltpu.VMEM)
    dma = pltpu.SemaphoreType.DMA
    rows, sums = pl.pallas_call(
        functools.partial(kernel, sizes, nodes_total),
        out_shape=(
            jax.ShapeDtypeStruct((VECS + PRIOR, ROWS * LANES), BF16),
            jax.ShapeDtypeStruct((VECS, LANES), F32),
        ),
        in_specs=[hbm] * (4 + TABLES),
        out_specs=(vmem, vmem),
        scratch_shapes=[pltpu.VMEM(t.shape, t.dtype) for t in tables]
        + [
            pltpu.VMEM((VECS, ROWS, LANES), BF16),
            pltpu.VMEM((PRIOR, ROWS, LANES), BF16),
            pltpu.VMEM((ROWS, LANES), BF16),
            pltpu.VMEM((ROWS, LANES), BF16),
            pltpu.VMEM((VECS, ROWS, LANES), BF16),
            pltpu.VMEM(low, BF16),
            pltpu.VMEM(low, BF16),
            pltpu.VMEM(high, BF16),
            pltpu.VMEM(high, BF16),
            pltpu.VMEM((2, CHUNKS, ROWS, LANES), BF16),
            pltpu.VMEM((2, CHUNKS, 80 * PAIRS, 2 * LANES), BF16),
            pltpu.VMEM((2, CHUNKS, 2, ROWS, LANES), BF16),
            pltpu.VMEM((6, ROWS, LANES), BF16),
            pltpu.VMEM((BLOCK, LANES), F32),
            pltpu.VMEM((ROWS, BLOCK), F32),
            pltpu.VMEM((ROWS, LANES), F32),
            pltpu.VMEM((16, ROWS, LANES), F32),
            pltpu.VMEM((PAIRS, BLOCK, 2 * LANES), BF16),
            pltpu.VMEM((CHUNK * ROWS, BLOCK), BF16),
            pltpu.VMEM((nz, 24, LANES), F32),
            pltpu.VMEM((nx, 24, LANES), F32),
            pltpu.VMEM((ny, 24, LANES), F32),
            dma((3 + CHUNKS + TABLES,)),
            dma((6,)),
            dma((2, CHUNKS, 2)),
            dma((2,)),
            dma((3,)),
            dma((3,)),
            pltpu.SemaphoreType.REGULAR((1,)),
        ],
        compiler_params=pltpu.CompilerParams(
            collective_id=0, has_side_effects=True, vmem_limit_bytes=24 * 2**20
        ),
    )(
        *[
            pltpu.with_memory_space_constraint(operand, pltpu.HBM)
            for operand in [
                panel_in.reshape(VECS, ROWS, LANES),
                prior_modes.reshape(PRIOR, ROWS, LANES),
                stiffness.reshape(ROWS, LANES),
                mass_shift.reshape(ROWS, LANES),
            ]
            + [jnp.asarray(t) for t in tables]
        ]
    )
    basis, upper = pl.pallas_call(
        functools.partial(finish_kernel, nodes_total),
        out_shape=(
            jax.ShapeDtypeStruct((VECS, ROWS, LANES), BF16),
            jax.ShapeDtypeStruct((VECS, VECS), F32),
        ),
        in_specs=[vmem, vmem],
        out_specs=(hbm, hbm),
        scratch_shapes=[
            pltpu.VMEM((VECS, ROWS, LANES), BF16),
            pltpu.VMEM((VECS, VECS), F32),
            dma((1 + SIDE // 2,)),
        ],
        compiler_params=pltpu.CompilerParams(vmem_limit_bytes=12 * 2**20),
    )(rows, sums)
    return basis.reshape(panel_in.shape), upper


def solution(mesh):
    sizes = tuple(mesh.shape[a] for a in ("gx", "gy", "gz"))
    nodes_total = ROWS * LANES * sizes[0] * sizes[1] * sizes[2]
    placed = (
        P(None, "gx", "gy", "gz"),
        P(None, "gx", "gy", "gz"),
        P("gx", "gy", "gz"),
        P("gx", "gy", "gz"),
    )
    return jax.shard_map(
        functools.partial(on_device, sizes, nodes_total),
        mesh=mesh,
        in_specs=placed,
        out_specs=(P(None, "gx", "gy", "gz"), P()),
        check_vma=False,
    )
```

```python
import functools

import jax
import jax.numpy as jnp
import ml_dtypes
import numpy as np
from jax import lax
from jax.experimental import pallas as pl
from jax.experimental.pallas import tpu as pltpu
from jax.sharding import PartitionSpec as P

filter_center = 10.0
filter_half = 12.0

MESH = pl.DeviceIdType.MESH
BF16 = jnp.bfloat16
F32 = jnp.float32
VECS = 32
PRIOR = 64
SIDE = 8
ROWS = SIDE * SIDE
LANES = 128
CHUNK = 4
CHUNKS = VECS // CHUNK
PAIRS = CHUNK // 2
SLOT = LANES // CHUNK
POINTS_Z = 5 * (LANES // 4 + 1)


def lobatto_tables():
    points = np.array([-1.0, -np.sqrt(3.0 / 7.0), 0.0, np.sqrt(3.0 / 7.0), 1.0])
    weights = np.array([0.1, 49.0 / 90.0, 32.0 / 45.0, 49.0 / 90.0, 0.1])
    scales = np.array(
        [np.prod([points[i] - points[k] for k in range(5) if k != i]) for i in range(5)]
    )
    derivative = np.zeros((5, 5))
    for i in range(5):
        for j in range(5):
            if j != i:
                derivative[i, j] = scales[i] / scales[j] / (points[i] - points[j])
        derivative[i, i] = -np.sum(derivative[i])
    return (derivative, weights)


def node_weight(count):
    weights = lobatto_tables()[1]
    per_node = [weights[3], weights[4] + weights[0], weights[1], weights[2]]
    return np.array([per_node[i % 4] for i in range(count)])


HIGH_X, HIGH_Y, LOW_X, LOW_Y = 64, 80, 96, 144
BLOCK = 256
LOW_X_R, LOW_Y_R, HIGH_Y_R = 0, 24 * PAIRS, 48 * PAIRS
LOW_Z_R, HIGH_Z_R, HIGH_X_R = 64 * PAIRS, 64 * PAIRS + 32, 64 * PAIRS + 64
FACE_ROWS = HIGH_X_R + 16 * PAIRS


def field_row(x, y, parity):
    if x < 0:
        return LOW_X + 24 * parity + (x + 3) * SIDE + y
    if y < 0:
        return LOW_Y + 24 * parity + (y + 3) * SIDE + x
    if x >= SIDE:
        return HIGH_X + (x - SIDE) * SIDE + y
    if y >= SIDE:
        return HIGH_Y + (y - SIDE) * SIDE + x
    return x * SIDE + y


def stiff_row(x, y):
    if x < 0:
        return ROWS + (x + SIDE) * SIDE + y
    if x >= SIDE:
        return 2 * ROWS + (x - SIDE) * SIDE + y
    if y < 0:
        return 3 * ROWS + x * SIDE + y + SIDE
    if y >= SIDE:
        return 4 * ROWS + x * SIDE + y - SIDE
    return x * SIDE + y


STIFF_K = 384


def make_tables():
    derivative, weights = lobatto_tables()
    node_w = node_weight(SIDE)
    node_z = node_weight(LANES)
    grad = np.zeros((2, BLOCK, BLOCK))
    back = np.zeros((ROWS, BLOCK))
    pick = np.zeros((BLOCK, STIFF_K))
    scale = np.zeros((BLOCK, LANES))
    for m in range(3):
        for q in range(5):
            for t in range(SIDE):
                rx = (m * 5 + q) * SIDE + t
                ry = 120 + rx
                at = 4 * m - 3 + q
                pick[rx, stiff_row(at, t)] = 1
                pick[ry, stiff_row(t, at)] = 1
                scale[rx] = weights[q] * node_w[t] * node_z
                scale[ry] = weights[q] * node_w[t] * node_z
                for a in range(5):
                    node = 4 * m - 3 + a
                    for parity in range(2):
                        grad[parity, rx, field_row(node, t, parity)] = derivative[q, a]
                        grad[parity, ry, field_row(t, node, parity)] = derivative[q, a]
                    if 0 <= node < SIDE:
                        back[node * SIDE + t, rx] = derivative[q, a]
                        back[t * SIDE + node, ry] = derivative[q, a]
    grad_z = np.zeros((2 * LANES, BLOCK))
    back_z = np.zeros((BLOCK, LANES))
    pick_z = np.zeros((3 * LANES, BLOCK))
    scale_z = np.zeros((ROWS, BLOCK))
    for m in range(LANES // 4 + 1):
        for q in range(5):
            col = 5 * m + q
            at = 4 * m - 3 + q
            source = at if 0 <= at < LANES else (2 * LANES + at if at < 0 else LANES + at)
            pick_z[source, col] = 1
            for t in range(ROWS):
                scale_z[t, col] = weights[q] * node_w[t // SIDE] * node_w[t % SIDE]
            for a in range(5):
                node = 4 * m - 3 + a
                row = node
                if node < 0:
                    row = LANES + node + 3
                elif node >= LANES:
                    row = LANES + 3 + node - LANES
                else:
                    back_z[col, node] = derivative[q, a]
                grad_z[row, col] = derivative[q, a]
    faces = np.zeros((128, 128))
    for half in range(2):
        for t in range(SIDE):
            for j in range(2):
                faces[16 * half + j * SIDE + t, 64 * half + t * SIDE + j] = 1
            for j in range(3):
                faces[32 + 24 * half + j * SIDE + t, 64 * half + (5 + j) * SIDE + t] = 1
                faces[80 + 24 * half + j * SIDE + t, 64 * half + t * SIDE + 5 + j] = 1
    volume = np.zeros((ROWS, LANES))
    for t in range(ROWS):
        volume[t] = node_w[t // SIDE] * node_w[t % SIDE] * node_z
    halves = [grad, back, pick, grad_z, back_z, pick_z, faces]
    singles = [scale, scale_z, volume]
    return [t.astype(np.float32).astype(ml_dtypes.bfloat16) for t in halves] + [
        t.astype(np.float32) for t in singles
    ]


def dot(a, b):
    return jnp.dot(a, b, preferred_element_type=F32)


def dot_nt(a, b, precision=None):
    return lax.dot_general(
        a, b, (((1,), (1,)), ((), ())), precision=precision, preferred_element_type=F32
    )


def side(shape, dim):
    return lax.broadcasted_iota(jnp.int32, shape, dim)


TABLES = 10


def kernel(sizes, nodes_total, *refs):
    panel, prior, stiff, mass = refs[:4]
    tables = refs[4 : 4 + TABLES]
    whole, sums_out = refs[4 + TABLES : 6 + TABLES]
    scratch = refs[6 + TABLES :]
    held = scratch[:TABLES]
    grad, back, pick, grad_z, back_z, pick_z, faces, scale, scale_z, volume = held
    (
        field,
        modes,
        stiff_own,
        mass_own,
        once,
        faces_s,
        faces_r,
        stiff_r,
        factor,
        factor_z,
        shift,
        image_rows,
        flux,
        flux_z,
        slots_z,
        slots_x,
        slots_y,
        load_sem,
        send_sem,
        recv_sem,
        stiff_sem,
        sum_send,
        sum_recv,
        token,
    ) = scratch[TABLES:]
    nx, ny, nz = sizes
    axes = ("gx", "gy", "gz")
    me = [lax.axis_index(a) for a in axes]

    def along(axis, step):
        return {axes[axis]: lax.rem(me[axis] + step + sizes[axis], sizes[axis])}

    barrier = pltpu.get_barrier_semaphore()

    def greet(semaphore):
        for axis in range(3):
            for step in (1, -1):
                pl.semaphore_signal(
                    semaphore, inc=1, device_id=along(axis, step), device_id_type=MESH
                )

    greet(barrier)
    loads = {}

    def load(name, src, dst):
        loads[name] = pltpu.make_async_copy(src, dst, load_sem.at[len(loads)])
        loads[name].start()

    def loaded(*names):
        for name in names:
            loads[name].wait()

    load("faces", tables[6], faces)
    load("stiff", stiff, stiff_own)
    for c in range(CHUNKS):
        part = pl.ds(c * CHUNK, CHUNK)
        load(c, panel.at[part], field.at[part])

    def pack(app, c, source):
        cells = [source[c * CHUNK + j] for j in range(CHUNK)]
        pairs = [
            jnp.concatenate([cells[2 * p], cells[2 * p + 1]], axis=1) for p in range(PAIRS)
        ]
        for p in range(PAIRS):
            at = HIGH_X_R + 16 * p
            faces_s[app, c, at : at + 16] = pairs[p][:16]
        for q in range(PAIRS // 2):
            both = jnp.concatenate([pairs[2 * q], pairs[2 * q + 1]], axis=0)
            picked = dot(faces[...], both).astype(BF16)
            for at, rows in (
                (HIGH_Y_R + 32 * q, picked[:32]),
                (LOW_X_R + 48 * q, picked[32:80]),
                (LOW_Y_R + 48 * q, picked[80:]),
            ):
                faces_s[app, c, at : at + rows.shape[0]] = rows
        lane = side((ROWS, LANES), 1)
        edges = jnp.zeros((ROWS, LANES), F32)
        for j in range(CHUNK):
            here = (lane >= SLOT * j) & (lane < SLOT * j + 5)
            edges = jnp.where(here, pltpu.roll(cells[j].astype(F32), SLOT * j + 3, 1), edges)
        edges = edges.astype(BF16)
        faces_s[app, c, LOW_Z_R : LOW_Z_R + 32] = jnp.concatenate(
            [edges[:32], edges[32:]], axis=1
        )

    first = [me[k] == 0 for k in range(3)]
    last = [me[k] == sizes[k] - 1 for k in range(3)]

    def one_of(condition, yes, no):
        return jnp.where(condition, yes, no).astype(jnp.int32)

    def crosses(axis, step):
        if axis != 0:
            return False
        return last[0] if step == 1 else first[0]

    def face_copies(app, c):
        plan = [
            (LOW_X_R, LOW_X_R, 24 * PAIRS, 0, 1),
            (HIGH_X_R, HIGH_X_R, 16 * PAIRS, 0, -1),
            (LOW_Y_R, LOW_Y_R, 24 * PAIRS, 1, 1),
            (HIGH_Y_R, HIGH_Y_R, 16 * PAIRS, 1, -1),
            (LOW_Z_R, LOW_Z_R, 32, 2, 1),
            (LOW_Z_R, HIGH_Z_R, 32, 2, -1),
        ]
        copies = []
        for here, there, rows, axis, step in plan:
            layer, signal = app, app * CHUNKS + c
            if axis == 0:
                aside = crosses(axis, step)
                layer = one_of(aside, app + 2, app)
                signal = one_of(aside, 2 * CHUNKS + (step < 0), signal)
            copies.append(
                pltpu.make_async_remote_copy(
                    src_ref=faces_s.at[app, c, pl.ds(here, rows)],
                    dst_ref=faces_r.at[layer, c, pl.ds(there, rows)],
                    send_sem=send_sem.at[0],
                    recv_sem=recv_sem.at[signal],
                    device_id=along(axis, step),
                    device_id_type=MESH,
                )
            )
        return copies

    def arrived(buffer, semaphore):
        pltpu.make_async_copy(buffer, buffer, semaphore).wait()

    inside = jnp.logical_not(first[0] | last[0])

    def arrived_inside(buffer, low, high, semaphore):
        rows = buffer.shape[0]
        for condition, start, end in (
            (inside, 0, rows),
            (first[0], low, rows),
            (last[0], 0, rows - high),
        ):

            @pl.when(condition)
            def _(start=start, end=end):
                arrived(buffer.at[pl.ds(start, end - start)], semaphore)

    def faces_arrived(app, c):
        arrived_inside(
            faces_r.at[app, c], 24 * PAIRS, 16 * PAIRS, recv_sem.at[app * CHUNKS + c]
        )

    def stiff_copies():
        copies = []
        for k, (axis, step) in enumerate(
            [(0, 1), (1, 1), (1, -1), (2, 1), (2, -1), (0, -1)]
        ):
            slot, signal = k, 1
            if axis == 0:
                aside = crosses(axis, step)
                slot, signal = one_of(aside, 6 + (step < 0), k), one_of(aside, 2, 1)
            copies.append(
                pltpu.make_async_remote_copy(
                    src_ref=stiff_own,
                    dst_ref=stiff_r.at[slot],
                    send_sem=stiff_sem.at[0],
                    recv_sem=stiff_sem.at[signal],
                    device_id=along(axis, step),
                    device_id_type=MESH,
                )
            )
        return copies

    loaded("faces", "stiff")
    for c in range(CHUNKS):
        loaded(c)
        if c == 0:
            for k in (0, 2, 3, 5, 7, 8, 9, 1, 4):
                load("table%d" % k, tables[k], held[k])
            load("mass", mass, mass_own)
            load("prior", prior, modes)
        pack(0, c, field)
        if c == 0:
            pl.semaphore_wait(barrier, 6)
            greet(token.at[0])
            for copy in stiff_copies():
                copy.start()
        for copy in face_copies(0, c):
            copy.start()

    loaded("table0", "table2", "table3", "table5")

    @pl.when(first[0])
    def _():
        stiff_r[0] = jnp.zeros((ROWS, LANES), BF16)
        for app in range(2):
            for c in range(CHUNKS):
                faces_r[app, c, :LOW_Y_R] = jnp.zeros((LOW_Y_R, 2 * LANES), BF16)

    @pl.when(last[0])
    def _():
        stiff_r[5] = jnp.zeros((ROWS, LANES), BF16)
        for app in range(2):
            for c in range(CHUNKS):
                faces_r[app, c, HIGH_X_R:] = jnp.zeros((16 * PAIRS, 2 * LANES), BF16)

    def outside(index, spans):
        cut = index < 0
        for low, high, missing in spans:
            cut = cut | ((index >= low) & (index < high) & missing)
        return cut

    col = side((BLOCK, BLOCK), 1)
    cut = outside(
        col,
        [
            (HIGH_X, HIGH_Y, last[0]),
            (HIGH_Y, LOW_X, last[1]),
            (LOW_X, LOW_Y, first[0]),
            (LOW_Y, LOW_Y + 48, first[1]),
        ],
    )
    for parity in range(2):
        grad[parity] = jnp.where(cut, 0.0, grad[parity].astype(F32)).astype(BF16)
    row = side((2 * LANES, BLOCK), 0)
    cut = outside(row, [(LANES, LANES + 3, first[2]), (LANES + 3, LANES + 5, last[2])])
    grad_z[...] = jnp.where(cut, 0.0, grad_z[...].astype(F32)).astype(BF16)
    col = side((BLOCK, STIFF_K), 1)
    cut = outside(
        col,
        [
            (ROWS, 2 * ROWS, first[0]),
            (2 * ROWS, 3 * ROWS, last[0]),
            (3 * ROWS, 4 * ROWS, first[1]),
            (4 * ROWS, 5 * ROWS, last[1]),
        ],
    )
    pick[...] = jnp.where(cut, 0.0, pick[...].astype(F32)).astype(BF16)
    row = side((3 * LANES, BLOCK), 0)
    cut = outside(row, [(LANES, 2 * LANES, first[2]), (2 * LANES, 3 * LANES, last[2])])
    pick_z[...] = jnp.where(cut, 0.0, pick_z[...].astype(F32)).astype(BF16)

    loaded("table7", "table8", "table9", "mass")
    shift[...] = volume[...] * mass_own[...].astype(F32) + filter_center

    loaded("table1", "table4", "prior")

    def place(at, cells):
        for x in range(SIDE):
            rows = slice(x * SIDE, (x + 1) * SIDE)
            block = jnp.stack([cell[rows] for cell in cells], axis=0)
            block = jnp.swapaxes(block, 0, 1).astype(BF16)
            for y in range(SIDE):
                first_lane = (x * SIDE + y) * LANES
                whole[at, first_lane : first_lane + LANES] = block[y]

    @pl.loop(0, PRIOR // 16)
    def _(g):
        at = pl.ds(pl.multiple_of(VECS + 16 * g, 16), 16)
        place(at, [modes[16 * g + j].astype(F32) for j in range(16)])

    arrived_inside(stiff_r.at[pl.ds(0, 6)], 1, 1, stiff_sem.at[1])
    around = jnp.concatenate(
        [stiff_own[...]]
        + [stiff_r[k] for k in (0, 5, 1, 2)]
        + [jnp.zeros((STIFF_K - 5 * ROWS, LANES), BF16)],
        axis=0,
    )
    factor[...] = dot(pick[...], around) * scale[...]
    around = jnp.concatenate([stiff_own[...], stiff_r[3], stiff_r[4]], axis=1)
    factor_z[...] = dot(around, pick_z[...]) * scale_z[...]

    def gradient(app, c, slot, source):
        lane = lax.rem(side((ROWS, LANES), 1), SLOT)
        ends = [faces_r[app, c, at : at + 32].astype(F32) for at in (LOW_Z_R, HIGH_Z_R)]
        low, high = [
            jnp.concatenate([end[:, :LANES], end[:, LANES:]], axis=0) for end in ends
        ]
        joined = jnp.where(lane < 3, low, high)
        cells = [source[c * CHUNK + j] for j in range(CHUNK)]
        lines = []
        for j in range(CHUNK):
            rolled = pltpu.roll(joined, LANES - SLOT * j, 1) if j else joined
            lines.append(jnp.concatenate([cells[j], rolled.astype(BF16)], axis=1))
        factor_rows = jnp.concatenate([factor_z[...]] * CHUNK, axis=0)
        flux_z[slot] = (
            dot(jnp.concatenate(lines, axis=0), grad_z[...]) * factor_rows
        ).astype(BF16)
        factor_two = jnp.concatenate([factor[...], factor[...]], axis=1)
        for p in range(PAIRS):
            q, parity = p // 2, p % 2

            def face(at, rows):
                return faces_r[app, c, at : at + rows]

            rows = jnp.concatenate(
                [
                    jnp.concatenate(cells[2 * p : 2 * p + 2], axis=1),
                    face(HIGH_X_R + 16 * p, 16),
                    face(HIGH_Y_R + 16 * p, 16),
                    face(LOW_X_R + 48 * q, 48),
                    face(LOW_Y_R + 48 * q, 48),
                    jnp.zeros((BLOCK - 192, 2 * LANES), BF16),
                ],
                axis=0,
            )
            flux[slot, p] = (dot(grad[parity], rows) * factor_two).astype(BF16)

    def divergence(c, slot, source, finish):
        image_z = dot(flux_z[slot], back_z[...])
        for p in range(PAIRS):
            image = dot(back[...], flux[slot, p])
            for h in range(2):
                j = 2 * p + h
                cell = source[c * CHUNK + j].astype(F32)
                moved = image[:, h * LANES : (h + 1) * LANES]
                moved = moved + image_z[j * ROWS : (j + 1) * ROWS] - shift[...] * cell
                finish(c * CHUNK + j, moved)

    def finish_one(j, moved):
        once[j] = (moved * (1.0 / filter_half)).astype(BF16)

    def finish_two(j, moved):
        done = moved * (2.0 / filter_half) - field[j].astype(F32)
        image_rows[lax.rem(j, 16)] = done

    group = 16 // CHUNK

    def send_once(c):
        pack(1, c, once)
        for copy in face_copies(1, c):
            copy.start()

    pl.semaphore_wait(token.at[0], 6)
    greet(token.at[1])

    @pl.loop(0, CHUNKS // group)
    def _(g):
        for k in range(group):
            c = g * group + k
            faces_arrived(0, c)
            if k > 0:
                divergence(c - 1, (k - 1) % 2, field, finish_one)
            gradient(0, c, k % 2, field)
            if k > 0:
                send_once(c - 1)
        c = g * group + group - 1
        divergence(c, (group - 1) % 2, field, finish_one)
        send_once(c)

    pl.semaphore_wait(token.at[1], 6)
    greet(token.at[2])

    @pl.loop(0, CHUNKS // group)
    def _(g):
        for k in range(group):
            c = g * group + k
            faces_arrived(1, c)
            if k > 0:
                divergence(c - 1, (k - 1) % 2, once, finish_two)
            gradient(1, c, k % 2, once)
        c = g * group + group - 1
        divergence(c, (group - 1) % 2, once, finish_two)
        at = pl.ds(pl.multiple_of(16 * g, 16), 16)
        place(at, [image_rows[j] for j in range(16)])

    sums = dot_nt(whole[:VECS], whole[...])
    sums = jnp.concatenate([sums, jnp.zeros((VECS, LANES - VECS - PRIOR), F32)], axis=1)

    lane = side((8, LANES), 1)
    used = VECS + PRIOR
    tail = sums[24:]
    mine = jnp.concatenate(
        [
            jnp.where(lane < used, sums[8 * r : 8 * r + 8], pltpu.roll(tail, used - 32 * r, 1))
            for r in range(3)
        ],
        axis=0,
    )
    pl.semaphore_wait(token.at[2], 6)
    for stage, (axis, slots) in enumerate(((2, slots_z), (0, slots_x), (1, slots_y))):
        size = sizes[axis]
        slots[0] = mine
        steps = sorted(range(1, size), key=lambda step: -min(step, size - step))
        for step in steps:
            pltpu.make_async_remote_copy(
                src_ref=slots.at[0],
                dst_ref=slots.at[step],
                send_sem=sum_send.at[stage],
                recv_sem=sum_recv.at[stage],
                device_id=along(axis, step),
                device_id_type=MESH,
            ).start()
        arrived(slots.at[pl.ds(1, size - 1)], sum_recv.at[stage])
        parts = [slots[lax.rem(me[axis] - k + size, size)] for k in range(size)]
        mine = parts[0]
        for part in parts[1:]:
            mine = mine + part
    tail = jnp.zeros((8, LANES), F32)
    for r in range(3):
        part = pltpu.roll(mine[8 * r : 8 * r + 8], LANES - used + 32 * r, 1)
        tail = jnp.where((lane >= 32 * r) & (lane < 32 * r + 32), part, tail)
    sums_out[...] = jnp.concatenate([mine, tail], axis=0)

    arrived(faces_r.at[pl.ds(0, 2)], send_sem.at[0])
    arrived(stiff_r.at[pl.ds(0, 6)], stiff_sem.at[0])

    @pl.when(first[0])
    def _():
        arrived(faces_r.at[pl.ds(2, 2), :, pl.ds(0, LOW_Y_R)], recv_sem.at[2 * CHUNKS])
        arrived(stiff_r.at[6], stiff_sem.at[2])

    @pl.when(last[0])
    def _():
        arrived(
            faces_r.at[pl.ds(2, 2), :, pl.ds(HIGH_X_R, 16 * PAIRS)],
            recv_sem.at[2 * CHUNKS + 1],
        )
        arrived(stiff_r.at[7], stiff_sem.at[2])

    for stage, slots in enumerate((slots_z, slots_x, slots_y)):
        arrived(slots.at[pl.ds(1, slots.shape[0] - 1)], sum_send.at[stage])


def finish_kernel(nodes_total, whole, sums_in, out, upper_out, result, upper, out_sem):
    lane = side((VECS, LANES), 1)
    line = side((VECS, LANES), 0)
    sums = sums_in[...] * (1.0 / nodes_total)
    proj = jnp.where((lane >= VECS) & (lane < VECS + PRIOR), sums, 0.0)
    coeffs = proj.astype(BF16)
    rest = proj - coeffs.astype(F32)
    rest_high = rest.astype(BF16)
    rest_low = (rest - rest_high.astype(F32)).astype(BF16)
    left = jnp.concatenate([coeffs, coeffs, coeffs, rest_high, rest_low], axis=1)
    right = jnp.concatenate([coeffs, rest_high, rest_low, coeffs, coeffs], axis=1)
    right = jnp.concatenate([right, jnp.zeros((LANES - VECS, 5 * LANES), BF16)], axis=0)
    state = jnp.where(lane < VECS, sums - dot_nt(left, right), 0.0)
    state = jnp.where(lane == line + VECS, 1.0, state)
    state = state - pltpu.roll(coeffs.astype(F32), VECS, 1)

    step = 8

    def rows_of(value):
        return jnp.concatenate([value] * (VECS // 8), axis=0)

    for first in range(0, VECS, step):
        cols = [
            jnp.broadcast_to(state[:, first + j : first + j + 1], (VECS, LANES))
            for j in range(step)
        ]
        lines = [
            jnp.broadcast_to(state[first + j : first + j + 1], (8, LANES)) for j in range(step)
        ]
        pivots = [
            [jnp.broadcast_to(cols[j][first + i : first + i + 1], (8, LANES)) for j in range(step)]
            for i in range(step)
        ]
        ratios = []
        for j in range(step):
            inverse = 1.0 / pivots[j][j]
            ratio = jnp.where(line > first + j, cols[j] * rows_of(inverse), 0.0)
            ratios.append(ratio)
            for i in range(j + 1, step):
                times = pivots[i][j] * inverse
                for t in range(j + 1, step):
                    pivots[i][t] = pivots[i][t] - times * pivots[j][t]
                lines[i] = lines[i] - times * lines[j]
                cols[i] = cols[i] - ratio * rows_of(pivots[j][i])
        for j in range(step):
            state = state - ratios[j] * rows_of(lines[j])
    diagonal = jnp.sum(jnp.where(lane == line, state, 0.0), axis=1, keepdims=True)
    state = state * (1.0 / jnp.sqrt(diagonal))
    upper[...] = jnp.where(lane >= line, state, 0.0)[:, :VECS]
    writes = [pltpu.make_async_copy(upper, upper_out, out_sem.at[0])]
    writes[0].start()

    solve = pltpu.roll(state, LANES - VECS, 1)[:, : VECS + PRIOR]
    high = solve.astype(BF16)
    low = (solve - high.astype(F32)).astype(BF16)
    solve = jnp.concatenate([high, low], axis=0)
    for k in range(SIDE // 2):
        blocks = []
        for x in (2 * k, 2 * k + 1):
            block = dot(solve, whole[:, x * SIDE * LANES : (x + 1) * SIDE * LANES])
            block = block[:VECS] + block[VECS:]
            block = jnp.stack(
                [block[:, y * LANES : (y + 1) * LANES] for y in range(SIDE)], axis=0
            )
            blocks.append(jnp.swapaxes(block, 0, 1))
        at = slice(2 * k * SIDE, 2 * (k + 1) * SIDE)
        for v in range(VECS):
            result[v, at] = jnp.concatenate([blocks[0][v], blocks[1][v]], axis=0).astype(BF16)
        part = pl.ds(2 * k * SIDE, 2 * SIDE)
        write = pltpu.make_async_copy(result.at[:, part], out.at[:, part], out_sem.at[1 + k])
        write.start()
        writes.append(write)
    for write in writes:
        write.wait()


def on_device(sizes, nodes_total, panel_in, prior_modes, stiffness, mass_shift):
    nx, ny, nz = sizes
    tables = make_tables()
    hbm = pl.BlockSpec(memory_space=pltpu.HBM)
    vmem = pl.BlockSpec(memory_space=pltpu.VMEM)
    dma = pltpu.SemaphoreType.DMA
    rows, sums = pl.pallas_call(
        functools.partial(kernel, sizes, nodes_total),
        out_shape=(
            jax.ShapeDtypeStruct((VECS + PRIOR, ROWS * LANES), BF16),
            jax.ShapeDtypeStruct((VECS, LANES), F32),
        ),
        in_specs=[hbm] * (4 + TABLES),
        out_specs=(vmem, vmem),
        scratch_shapes=[pltpu.VMEM(t.shape, t.dtype) for t in tables]
        + [
            pltpu.VMEM((VECS, ROWS, LANES), BF16),
            pltpu.VMEM((PRIOR, ROWS, LANES), BF16),
            pltpu.VMEM((ROWS, LANES), BF16),
            pltpu.VMEM((ROWS, LANES), BF16),
            pltpu.VMEM((VECS, ROWS, LANES), BF16),
            pltpu.VMEM((2, CHUNKS, FACE_ROWS, 2 * LANES), BF16),
            pltpu.VMEM((4, CHUNKS, FACE_ROWS, 2 * LANES), BF16),
            pltpu.VMEM((8, ROWS, LANES), BF16),
            pltpu.VMEM((BLOCK, LANES), F32),
            pltpu.VMEM((ROWS, BLOCK), F32),
            pltpu.VMEM((ROWS, LANES), F32),
            pltpu.VMEM((16, ROWS, LANES), F32),
            pltpu.VMEM((2, PAIRS, BLOCK, 2 * LANES), BF16),
            pltpu.VMEM((2, CHUNK * ROWS, BLOCK), BF16),
            pltpu.VMEM((nz, 24, LANES), F32),
            pltpu.VMEM((nx, 24, LANES), F32),
            pltpu.VMEM((ny, 24, LANES), F32),
            dma((3 + CHUNKS + TABLES,)),
            dma((1,)),
            dma((2 * CHUNKS + 2,)),
            dma((3,)),
            dma((3,)),
            dma((3,)),
            pltpu.SemaphoreType.REGULAR((3,)),
        ],
        compiler_params=pltpu.CompilerParams(
            collective_id=0, has_side_effects=True, vmem_limit_bytes=24 * 2**20
        ),
    )(
        *[
            pltpu.with_memory_space_constraint(operand, pltpu.HBM)
            for operand in [
                panel_in.reshape(VECS, ROWS, LANES),
                prior_modes.reshape(PRIOR, ROWS, LANES),
                stiffness.reshape(ROWS, LANES),
                mass_shift.reshape(ROWS, LANES),
            ]
            + [jnp.asarray(t) for t in tables]
        ]
    )
    basis, upper = pl.pallas_call(
        functools.partial(finish_kernel, nodes_total),
        out_shape=(
            jax.ShapeDtypeStruct((VECS, ROWS, LANES), BF16),
            jax.ShapeDtypeStruct((VECS, VECS), F32),
        ),
        in_specs=[vmem, vmem],
        out_specs=(hbm, hbm),
        scratch_shapes=[
            pltpu.VMEM((VECS, ROWS, LANES), BF16),
            pltpu.VMEM((VECS, VECS), F32),
            dma((1 + SIDE // 2,)),
        ],
        compiler_params=pltpu.CompilerParams(vmem_limit_bytes=12 * 2**20),
    )(rows, sums)
    return basis.reshape(panel_in.shape), upper


def solution(mesh):
    sizes = tuple(mesh.shape[a] for a in ("gx", "gy", "gz"))
    nodes_total = ROWS * LANES * sizes[0] * sizes[1] * sizes[2]
    placed = (
        P(None, "gx", "gy", "gz"),
        P(None, "gx", "gy", "gz"),
        P("gx", "gy", "gz"),
        P("gx", "gy", "gz"),
    )
    return jax.shard_map(
        functools.partial(on_device, sizes, nodes_total),
        mesh=mesh,
        in_specs=placed,
        out_specs=(P(None, "gx", "gy", "gz"), P()),
        check_vma=False,
    )
```
